256 devices in a mesh: amp: 64 (over y, z, core), ctr: 4 (over x).
Axes of the slice: x: 4, y: 4, z: 8, core: 2. Of those that a mesh axis runs over, the one named last changes fastest.
Arguments:
- amplitudes: bfloat16 [4, 768, 64, 768], P(None, 'amp', 'ctr'), may hold values from -6 to 6
- integrals: bfloat16 [64, 768, 2, 768], P('ctr', 'amp'), may hold values from -0.078125 to 0.078125
- occ_irrep: int32 [64], replicated, may hold values from 0 to 7
- vir_irrep: int32 [768], replicated, may hold values from 0 to 7
Outputs:
- cycle_term: float32 [4, 768, 2, 768], P('ctr', 'amp')
The draws below stay inside these ranges and needn't reach their ends.
Inputs may be any that keep to these rules, and one draw needn't show every extreme that they name: `occ_irrep`: D2h irrep labels. `vir_irrep`: D2h irrep labels.
All inputs are finite; a program needn't handle non-finite values.
Results may differ from the reference program's by a relative error of at most 0.0003.
Values may be sent and summed in bfloat16 or wider, within the bound.
A program may use at most 256 MiB of HBM per device.

```python
import math
import jax
import jax.numpy as jnp
import numpy as np
from jax import lax

O = 64
V = 768
J = 2
ITILE = 4


def plant(array, own_key, low, high):
    longest = array.shape.index(max(array.shape))
    spots = []
    for shift in (0, 1):
        where = [jax.random.randint(jax.random.fold_in(own_key, axis), (), 0, length) for axis, length in enumerate(array.shape)]
        where[longest] = (where[longest] + shift) % array.shape[longest]
        spots.append(tuple(where))
    return array.at[spots[0]].set(low).at[spots[1]].set(high)


def level_of(stream_key, extent, split, least, top_value):
    def one(axis_at, blocks):
        steps = jax.random.uniform(jax.random.fold_in(jax.random.fold_in(stream_key, 6), axis_at), (blocks,), jnp.float32, least / len(split), top_value / len(split))
        return jnp.repeat(jnp.exp(steps), extent[axis_at] // blocks).reshape((-1,) + (1,) * (len(extent) - axis_at - 1))

    level = one(*split[0])
    for cut in split[1:]:
        level = level * one(*cut)
    return level


def rank_table(number_of, skew):
    weights = [(1 << 20) // math.isqrt(standing ** skew) + 1 for standing in range(1, number_of + 1)]
    width = 1 + sum(weights) // (1 << 30)
    return np.cumsum(np.array([max(1, weight // width) for weight in weights]))


def ranked(key, shape, amount, lean):
    listing = rank_table(amount, lean)
    ticket = jax.random.randint(jax.random.fold_in(key, 1), shape, 0, int(listing[amount - 1]))
    rank = jnp.searchsorted(jnp.asarray(listing, jnp.int32), ticket, side="right")
    return jax.random.permutation(jax.random.fold_in(key, 2), amount)[rank].astype(jnp.int32)


def gaussian(key, shape, spread, limit, shards=(), held_as=jnp.bfloat16):
    array = jax.random.normal(key, shape, jnp.float32) * spread
    if len(shards) > 0:
        array = level_of(key, shape, shards, -0.22, 0.18) * array
    return jnp.clip(array, min=-limit, max=limit).astype(held_as)


def setup_inputs(seed: int = 0) -> dict:
    splits = jax.random.split(jax.random.key(seed), 5)
    return {
        "amplitudes": gaussian(splits[0], (ITILE, V, O, V), 1.0, 6.0, ((1, 64), (2, 4))),
        "integrals": gaussian(splits[1], (O, V, J, V), (O * V // 8) ** -0.5, 0.078125, ((0, 4), (1, 64))),
        "occ_irrep": plant(ranked(splits[2], (O,), 8, 1), jax.random.fold_in(splits[2], 3), 0, 7).astype(jnp.int32),
        "vir_irrep": plant(ranked(splits[3], (V,), 8, 1), jax.random.fold_in(splits[3], 3), 0, 7).astype(jnp.int32),
    }


def reference(amplitudes, integrals, occ_irrep, vir_irrep):
    tile_labels = occ_irrep[:ITILE]
    pair_labels = occ_irrep[ITILE:ITILE + J]
    w_left = jnp.bitwise_xor(occ_irrep[:, None, None, None], vir_irrep[None, :, None, None])
    w_right = jnp.bitwise_xor(pair_labels[None, None, :, None], vir_irrep[None, None, None, :])
    w_masked = jnp.where(w_left == w_right, integrals, jnp.zeros_like(integrals))
    w_matrix = w_masked.astype(jnp.float32).reshape(O * V, J * V)
    kc_labels = jnp.bitwise_xor(occ_irrep[None, :, None], vir_irrep[None, None, :])

    def one_row(packed):
        rows, label = packed
        row_labels = jnp.bitwise_xor(label, vir_irrep)[:, None, None]
        masked = jnp.where(row_labels == kc_labels, rows, jnp.zeros_like(rows))
        left = masked.astype(jnp.float32).reshape(V, O * V)
        return jnp.dot(left, w_matrix, precision=lax.Precision.HIGHEST, preferred_element_type=jnp.float32).reshape(V, J, V)

    contracted = lax.map(one_row, (amplitudes, tile_labels))
    return contracted + jnp.transpose(contracted, (0, 3, 2, 1))
```

```python
import functools

import jax
import jax.numpy as jnp
from jax import lax
from jax.experimental import pallas as pl
from jax.experimental.pallas import tpu as pltpu
from jax.sharding import PartitionSpec as P

O, V, ITILE, J = 64, 768, 4, 2
NX, NCHIP, AB = 4, 32, 12
KB = O // NX
CAPB = 256
CAPK = 21
MESH = pl.DeviceIdType.MESH
F32, BF16, I32 = jnp.float32, jnp.bfloat16, jnp.int32
NT = (((1,), (1,)), ((), ()))


def dense_shards(amplitudes, integrals, occ_irrep, vir_irrep):
    regrouped = lax.all_to_all(
        lax.all_to_all(amplitudes, "amp", split_axis=3, concat_axis=1, tiled=True),
        "ctr",
        split_axis=0,
        concat_axis=2,
        tiled=True,
    )
    own_rows, vir_full, occ_full, vir_local = regrouped.shape
    tile_size = own_rows * lax.axis_size("ctr")
    pair_count = integrals.shape[2]
    vir_block = lax.dynamic_slice_in_dim(vir_irrep, lax.axis_index("amp") * vir_local, vir_local)
    occ_tile = lax.dynamic_slice_in_dim(occ_irrep, lax.axis_index("ctr") * own_rows, own_rows)
    pair_labels = lax.dynamic_slice_in_dim(occ_irrep, tile_size, pair_count)
    t_left = jnp.bitwise_xor(occ_tile[:, None, None, None], vir_irrep[None, :, None, None])
    t_right = jnp.bitwise_xor(occ_irrep[None, None, :, None], vir_block[None, None, None, :])
    masked_amps = jnp.where(t_left == t_right, regrouped, jnp.zeros_like(regrouped))
    amp_matrix = masked_amps.reshape(own_rows * vir_full, occ_full * vir_local)
    w_right = jnp.bitwise_xor(pair_labels[None, None, :, None], vir_irrep[None, None, None, :])
    integral_block = lax.all_gather(integrals, "ctr", axis=0, tiled=True)
    count = integral_block.shape[0]
    w_left = jnp.bitwise_xor(occ_irrep[:, None, None, None], vir_block[None, :, None, None])
    w_masked = jnp.where(w_left == w_right, integral_block, jnp.zeros_like(integral_block))
    w_matrix = w_masked.reshape(count * vir_local, pair_count * vir_full)
    partial_value = jnp.dot(amp_matrix, w_matrix, preferred_element_type=jnp.float32)
    partial_value = partial_value.reshape(own_rows, vir_full, pair_count, vir_full)
    summed = lax.psum_scatter(partial_value, "amp", scatter_dimension=1, tiled=True)
    swapped = lax.all_to_all(summed, "amp", split_axis=3, concat_axis=1, tiled=True)
    return summed + jnp.transpose(swapped, (0, 3, 2, 1))


def iota(shape, dim):
    return lax.broadcasted_iota(I32, shape, dim)


def onehot(cond):
    return jnp.where(cond, 1.0, 0.0).astype(BF16)


def split2(value):
    hi = value.astype(BF16)
    return hi, (value - hi.astype(F32)).astype(BF16)


def kernel(
    t_ref, w_ref, occ_ref, virc_ref, virr_ref, out_ref,
    q_ref, cols_ref, rows_ref, rt_ref, rbd_ref, tps, tpr, ws, wb, ut, lhs6, msgf, msg, rxa, rxb, rxf,
    ls, rs, sp, rsrx, x2s, x2r,
    t_ss, t_rs, w_ss, w_rs, m_ss, m_rs, f_ss, f_rs, r_ss, r_rs, x_ss, x_rs,
):
    amp = lax.axis_index("amp")
    x = lax.axis_index("ctr")
    chip, core = amp // 2, amp % 2
    sib = 1 - core

    barrier = pltpu.get_barrier_semaphore()

    @pl.loop(1, NCHIP)
    def _(d):
        q = lax.rem(chip + d, NCHIP)
        pl.semaphore_signal(barrier, inc=1, device_id=(q * 2 + core, x), device_id_type=MESH)

    for d in range(1, 8):
        xx = lax.rem(x + d // 2, NX)
        cc = core if d % 2 == 0 else sib
        pl.semaphore_signal(barrier, inc=1, device_id=(chip * 2 + cc, xx), device_id_type=MESH)

    occ8 = occ_ref[...]
    occ_i = [occ8[0:1, r : r + 1] for r in range(ITILE)]
    occ_j = [occ8[0:1, ITILE + r : ITILE + r + 1] for r in range(J)]
    own_i = jnp.where(x < 2, jnp.where(x == 0, occ_i[0], occ_i[1]), jnp.where(x == 2, occ_i[2], occ_i[3]))
    own_j = jnp.where(core == 0, occ_j[0], occ_j[1])
    occ_sq = jnp.broadcast_to(occ8[0:1, :], (128, 128))
    occ_cl = occ_sq.T
    r0, r1 = iota((128, 128), 0), iota((128, 128), 1)
    rank_k = jnp.sum(jnp.where((occ_sq == occ_cl) & (r0 < r1) & (r0 < O), 1.0, 0.0), axis=0, keepdims=True)
    vchip = virc_ref[pl.ds(chip, 1), :]
    sub8 = iota((8, 128), 0)
    table = jnp.where(
        sub8 == 0,
        occ8.astype(F32),
        jnp.where(sub8 == 1, jnp.broadcast_to(vchip, (8, 128)).astype(F32), jnp.broadcast_to(rank_k, (8, 128))),
    ).astype(BF16)
    lane = iota((1, V), 1)
    deep = iota((128, V), 0)

    def expand(index):
        return jnp.dot(table, onehot(deep == index), preferred_element_type=F32).astype(I32)

    def occ_at(e):
        return e[0:1]

    def vir_at(e):
        return e[1:2]

    def rank_at(e):
        return e[2:3]

    vrow = virr_ref[0:1, :]
    lane_i = lane // (AB * KB)
    lab_i = jnp.where(lane_i < 2, jnp.where(lane_i == 0, occ_i[0], occ_i[1]), jnp.where(lane_i == 2, occ_i[2], occ_i[3]))
    row_t = lab_i ^ occ_at(expand(x * KB + lane % KB)) ^ vir_at(expand(core * AB + (lane % (AB * KB)) // KB))
    e_k = expand(lane % O)
    row_ak = own_i ^ occ_at(e_k) ^ vir_at(expand(core * AB + lane // O))
    e_kc = expand(lane // AB)
    c0 = vir_at(expand(lane % AB))
    c1 = vir_at(expand(AB + lane % AB))
    own_c = jnp.where(core == 0, c0, c1)
    row_w = occ_at(expand(x * KB + lane // AB)) ^ own_c
    rows_ref[0:1, :] = row_ak
    rows_ref[1:2, :] = occ_at(e_kc) ^ c0 ^ own_j
    rows_ref[2:3, :] = occ_at(e_kc) ^ c1 ^ own_j
    stack = jnp.concatenate(
        [row_t, row_w, rank_at(e_k), rank_at(e_kc), vrow, own_c, vrow, vrow], axis=0
    )
    cols_ref[...] = jnp.concatenate([stack] * 16, axis=0).T
    vcol = cols_ref[:, 4:5]
    same = jnp.where(vcol == iota((V, 128), 1), 1.0, 0.0)
    lower = onehot(iota((V, V), 0) > iota((V, V), 1))
    counts = jnp.dot(lower, same.astype(BF16), preferred_element_type=F32)
    rank = jnp.sum(counts * same, axis=1, keepdims=True).astype(I32)
    q_ref[...] = onehot(rank == iota((V, CAPB), 1))

    @pl.loop(0, ITILE)
    def _(i):
        rows = pl.ds(pl.multiple_of(i * AB * KB, AB * KB), AB * KB)
        keep = cols_ref[rows, 0:1] == virr_ref[0:1, :]
        masked = jnp.where(keep, t_ref[rows, :].astype(F32), 0.0).astype(BF16)
        packed = jnp.dot(masked, q_ref[...], preferred_element_type=F32).astype(BF16)
        tps[i] = packed.reshape(AB, KB, CAPB)

    pl.semaphore_wait(barrier, NCHIP - 1 + 7)

    def t_copy(xx, slot):
        return pltpu.make_async_remote_copy(
            src_ref=tps.at[xx], dst_ref=tpr.at[:, slot], send_sem=t_ss.at[xx], recv_sem=t_rs.at[slot],
            device_id=(amp, xx), device_id_type=MESH,
        )

    for d in range(1, NX):
        t_copy(lax.rem(x + d, NX), x).start()
    tpr[:, x] = tps[x]

    for j in range(J):
        keep = (cols_ref[0 : KB * AB, 1:2] ^ occ_j[j]) == virr_ref[0:1, :]
        masked = jnp.where(keep, w_ref[j].astype(F32), 0.0).astype(BF16)
        ws[j] = jnp.dot(masked, q_ref[...], preferred_element_type=F32).astype(BF16)

    def w_copy(xx, cc, slot_x, slot_c):
        return pltpu.make_async_remote_copy(
            src_ref=ws.at[cc], dst_ref=wb.at[slot_c, slot_x], send_sem=w_ss.at[cc, xx], recv_sem=w_rs.at[slot_c, slot_x],
            device_id=(chip * 2 + cc, xx), device_id_type=MESH,
        )

    for d in range(1, 8):
        w_copy(lax.rem(x + d // 2, NX), core if d % 2 == 0 else sib, x, core).start()
    wb[core, x] = ws[core]

    pair = iota((V, 256), 1)
    inner = pair % 128
    deep_t = iota((V, 256), 0)
    rt_ref[...] = onehot(
        (inner // CAPK == deep_t // 128)
        & (pair // 128 == (deep_t % 128) // O)
        & (inner % CAPK == cols_ref[:, 2:3])
        & (inner < 6 * CAPK)
    )
    rbd_ref[...] = onehot(
        ((pair // 128) * 6 + inner // CAPK == deep_t % AB)
        & (inner % CAPK == cols_ref[:, 3:4])
        & (inner < 6 * CAPK)
    )

    for d in range(1, NX):
        xx = lax.rem(x + d, NX)
        t_copy(xx, xx).wait_recv()

    @pl.loop(0, 6)
    def _(m):
        rows = pl.ds(pl.multiple_of(m * 128, 128), 128)
        full = lax.dot_general(q_ref[rows, :], tpr[...].reshape(V, CAPB), NT, preferred_element_type=F32)
        full = jnp.where(cols_ref[rows, 4:5] == rows_ref[0:1, :], full, 0.0)
        for t in range(6):
            ut[t, rows, :] = full[:, t * 128 : (t + 1) * 128]

    @pl.loop(0, 4)
    def _(g):
        for t in range(6):
            for c6 in range(6):
                piece = ut[t, pl.ds(g * 6 + c6, NCHIP, stride=24), :]
                lhs6[t * NCHIP : (t + 1) * NCHIP, c6 * 128 : (c6 + 1) * 128] = piece.astype(BF16)
        packed = jnp.dot(lhs6[...], rt_ref[...], preferred_element_type=F32)
        for t in range(6):
            for a2 in range(2):
                msgf[pl.ds((2 * t + a2) * 4 + g, NCHIP, stride=48), :] = packed[
                    t * NCHIP : (t + 1) * NCHIP, a2 * 128 : (a2 + 1) * 128
                ]

    msg[...] = msgf[...].astype(BF16).reshape(NCHIP, 48, 128)

    def m_copy(q, slot):
        return pltpu.make_async_remote_copy(
            src_ref=msg.at[q], dst_ref=rxa.at[slot], send_sem=m_ss.at[q], recv_sem=m_rs.at[slot],
            device_id=(q * 2 + core, x), device_id_type=MESH,
        )

    @pl.loop(1, NCHIP)
    def _(d):
        m_copy(lax.rem(chip + d, NCHIP), chip).start()

    rxa[chip] = msg[chip]

    for d in range(1, 8):
        xx, cc = lax.rem(x + d // 2, NX), core if d % 2 == 0 else sib
        w_copy(xx, cc, xx, cc).wait_recv()

    @pl.loop(0, 6)
    def _(m):
        rows = pl.ds(pl.multiple_of(m * 128, 128), 128)
        for c in range(2):
            block = wb[c].reshape(V, CAPB)
            full = lax.dot_general(q_ref[rows, :], block, NT, preferred_element_type=F32)
            full = jnp.where(cols_ref[rows, 4:5] == rows_ref[1 + c : 2 + c, :], full, 0.0).astype(BF16)
            packed = jnp.dot(full, rbd_ref[...], preferred_element_type=F32).astype(BF16)
            ls[rows, 512 + c * 256 : 768 + c * 256] = packed
            rs[rows, c * 256 : (c + 1) * 256] = packed

    @pl.loop(1, NCHIP)
    def _(d):
        q = lax.rem(chip + d, NCHIP)
        m_copy(q, q).wait_recv()

    forward = pltpu.make_async_remote_copy(
        src_ref=rxa, dst_ref=rxb, send_sem=f_ss, recv_sem=f_rs, device_id=(chip * 2 + sib, x), device_id_type=MESH
    )
    forward.start()

    @pl.loop(0, NCHIP)
    def _(q):
        rxf[pl.ds(pl.multiple_of((q * 2 + core) * 48, 48), 48), :] = rxa[q].astype(F32)

    forward.wait_recv()

    @pl.loop(0, NCHIP)
    def _(q):
        rxf[pl.ds(pl.multiple_of((q * 2 + sib) * 48, 48), 48), :] = rxb[q].astype(F32)

    for g in range(4):
        piece = rxf[pl.ds(g, V, stride=4), :].astype(BF16)
        ls[:, g * 128 : (g + 1) * 128] = piece
        rs[:, 512 + g * 128 : 640 + g * 128] = piece

    def r_copy(q, slot):
        return pltpu.make_async_remote_copy(
            src_ref=sp.at[q], dst_ref=rsrx.at[slot], send_sem=r_ss.at[q], recv_sem=r_rs.at[slot],
            device_id=(q * 2 + core, x), device_id_type=MESH,
        )

    for step in range(1, 5):
        yy = lax.rem(chip // 8 + step, 4)
        rows = pl.ds(pl.multiple_of(yy * 192, 192), 192)
        full = lax.dot_general(ls[rows, :], rs[...], NT, preferred_element_type=F32)
        keep = cols_ref[rows, 4:5] == (virr_ref[0:1, :] ^ (own_i ^ own_j))
        hi, lo = split2(jnp.where(keep, full, 0.0))
        packed = jnp.dot(hi, q_ref[...], preferred_element_type=F32)
        packed += jnp.dot(lo, q_ref[...], preferred_element_type=F32)
        sp[pl.ds(yy * 8, 8)] = packed.reshape(8, 24, CAPB)

        @pl.loop(0, 8)
        def _(d):
            q = yy * 8 + lax.rem(chip + 1 + d, 8)

            @pl.when(q != chip)
            def _():
                r_copy(q, chip).start()

    rsrx[chip] = sp[chip]

    @pl.loop(1, NCHIP)
    def _(d):
        q = lax.rem(chip + d, NCHIP)
        r_copy(q, q).wait_recv()

    total = jnp.sum(rsrx[...], axis=0)
    first, second = total[0:AB], total[AB : 2 * AB]
    x2s[...] = jnp.concatenate([jnp.where(core == 0, second, first), jnp.zeros((4, CAPB), F32)], axis=0)
    swap = pltpu.make_async_remote_copy(
        src_ref=x2s, dst_ref=x2r, send_sem=x_ss, recv_sem=x_rs, device_id=(chip * 2 + sib, x), device_id_type=MESH
    )
    swap.start()
    mine = jnp.where(core == 0, first, second)
    swap.wait_recv()
    other = x2r[0:AB, :]
    for j in range(J):
        hi, lo = split2(jnp.where(core == j, mine, other))
        full = lax.dot_general(hi, q_ref[...], NT, preferred_element_type=F32)
        full += lax.dot_general(lo, q_ref[...], NT, preferred_element_type=F32)
        keep = cols_ref[0:AB, 5:6] == (virr_ref[0:1, :] ^ (own_i ^ occ_j[j]))
        out_ref[:, j, :] = jnp.where(keep, full, 0.0)

    for d in range(1, NX):
        t_copy(lax.rem(x + d, NX), x).wait_send()
    for d in range(1, 8):
        w_copy(lax.rem(x + d // 2, NX), core if d % 2 == 0 else sib, x, core).wait_send()
    forward.wait_send()
    swap.wait_send()

    @pl.loop(1, NCHIP)
    def _(d):
        q = lax.rem(chip + d, NCHIP)
        m_copy(q, chip).wait_send()
        r_copy(q, chip).wait_send()


def packed_shards(amplitudes, integrals, occ_irrep, vir_irrep):
    t = amplitudes.reshape(ITILE * AB * KB, V)
    w = jnp.transpose(integrals, (2, 0, 1, 3)).reshape(J, KB * AB, V)
    occ8 = jnp.broadcast_to(jnp.pad(occ_irrep, (0, 128 - O))[None, :], (8, 128))
    virc = jnp.pad(vir_irrep.reshape(NCHIP, 2 * AB), ((0, 0), (0, 128 - 2 * AB)))
    virr = jnp.broadcast_to(vir_irrep[None, :], (8, V))
    vm = pltpu.VMEM
    dma = pltpu.SemaphoreType.DMA
    out = pl.pallas_call(
        kernel,
        out_shape=jax.ShapeDtypeStruct((AB, J, V), F32),
        in_specs=[pl.BlockSpec(memory_space=vm)] * 5,
        out_specs=pl.BlockSpec(memory_space=vm),
        scratch_shapes=[
            vm((V, CAPB), BF16), vm((V, 128), I32), vm((8, V), I32), vm((V, 256), BF16), vm((V, 256), BF16),
            vm((ITILE, AB, KB, CAPB), BF16), vm((AB, NX, KB, CAPB), BF16),
            vm((J, KB * AB, CAPB), BF16), vm((2, NX, KB * AB, CAPB), BF16),
            vm((6, V, 128), F32), vm((6 * NCHIP, V), BF16), vm((NCHIP * 48, 128), F32),
            vm((NCHIP, 48, 128), BF16), vm((NCHIP, 48, 128), BF16), vm((NCHIP, 48, 128), BF16),
            vm((2 * NCHIP * 48, 128), F32),
            vm((V, 1024), BF16), vm((V, 1024), BF16),
            vm((NCHIP, 24, CAPB), F32), vm((NCHIP, 24, CAPB), F32), vm((16, CAPB), F32), vm((16, CAPB), F32),
            dma((NX,)), dma((NX,)), dma((2, NX)), dma((2, NX)), dma((NCHIP,)), dma((NCHIP,)),
            dma, dma, dma((NCHIP,)), dma((NCHIP,)), dma, dma,
        ],
        compiler_params=pltpu.CompilerParams(
            collective_id=0, has_side_effects=True, vmem_limit_bytes=48 * 1024 * 1024
        ),
        cost_estimate=pl.CostEstimate(flops=6_000_000_000, bytes_accessed=4_000_000, transcendentals=0),
    )(t, w, occ8, virc, virr)
    return out[None]


def shards(amplitudes, integrals, occ_irrep, vir_irrep):
    irreps = jnp.arange(8, dtype=I32)
    occ_top = jnp.max(jnp.sum((occ_irrep[None, :] == irreps[:, None]).astype(I32), axis=1))
    vir_top = jnp.max(jnp.sum((vir_irrep[None, :] == irreps[:, None]).astype(I32), axis=1))
    fits = (occ_top <= CAPK) & (vir_top <= CAPB)
    return lax.cond(fits, packed_shards, dense_shards, amplitudes, integrals, occ_irrep, vir_irrep)


def solution(mesh):
    return jax.shard_map(
        shards,
        mesh=mesh,
        in_specs=(P(None, "amp", "ctr", None), P("ctr", "amp", None, None), P(), P()),
        out_specs=P("ctr", "amp", None, None),
        check_vma=False,
    )
```

```python
import functools

import jax
import jax.numpy as jnp
from jax import lax
from jax.experimental import pallas as pl
from jax.experimental.pallas import tpu as pltpu
from jax.sharding import PartitionSpec as P

O, V, ITILE, J = 64, 768, 4, 2
NX, NCHIP, AB = 4, 32, 12
KB = O // NX
CAPB = 192
CAPK = 21
MESH = pl.DeviceIdType.MESH
F32, BF16, I32 = jnp.float32, jnp.bfloat16, jnp.int32
NT = (((1,), (1,)), ((), ()))


def dense_shards(amplitudes, integrals, occ_irrep, vir_irrep):
    regrouped = lax.all_to_all(
        lax.all_to_all(amplitudes, "amp", split_axis=3, concat_axis=1, tiled=True),
        "ctr",
        split_axis=0,
        concat_axis=2,
        tiled=True,
    )
    own_rows, vir_full, occ_full, vir_local = regrouped.shape
    tile_size = own_rows * lax.axis_size("ctr")
    pair_count = integrals.shape[2]
    vir_block = lax.dynamic_slice_in_dim(vir_irrep, lax.axis_index("amp") * vir_local, vir_local)
    occ_tile = lax.dynamic_slice_in_dim(occ_irrep, lax.axis_index("ctr") * own_rows, own_rows)
    pair_labels = lax.dynamic_slice_in_dim(occ_irrep, tile_size, pair_count)
    t_left = jnp.bitwise_xor(occ_tile[:, None, None, None], vir_irrep[None, :, None, None])
    t_right = jnp.bitwise_xor(occ_irrep[None, None, :, None], vir_block[None, None, None, :])
    masked_amps = jnp.where(t_left == t_right, regrouped, jnp.zeros_like(regrouped))
    amp_matrix = masked_amps.reshape(own_rows * vir_full, occ_full * vir_local)
    w_right = jnp.bitwise_xor(pair_labels[None, None, :, None], vir_irrep[None, None, None, :])
    copies = jnp.broadcast_to(integrals[None], (lax.axis_size("ctr"),) + integrals.shape)
    integral_block = lax.all_to_all(copies, "ctr", split_axis=0, concat_axis=0, tiled=True)
    integral_block = integral_block.reshape((-1,) + integrals.shape[1:])
    count = integral_block.shape[0]
    w_left = jnp.bitwise_xor(occ_irrep[:, None, None, None], vir_block[None, :, None, None])
    w_masked = jnp.where(w_left == w_right, integral_block, jnp.zeros_like(integral_block))
    w_matrix = w_masked.reshape(count * vir_local, pair_count * vir_full)
    partial_value = jnp.dot(amp_matrix, w_matrix, preferred_element_type=jnp.float32)
    partial_value = partial_value.reshape(own_rows, vir_full, pair_count, vir_full)
    pieces = partial_value.reshape(lax.axis_size("amp"), own_rows, vir_local, pair_count, vir_full)
    summed = jnp.sum(lax.all_to_all(pieces, "amp", split_axis=0, concat_axis=0, tiled=True), axis=0)
    swapped = lax.all_to_all(summed, "amp", split_axis=3, concat_axis=1, tiled=True)
    return summed + jnp.transpose(swapped, (0, 3, 2, 1))


def iota(shape, dim):
    return lax.broadcasted_iota(I32, shape, dim)


def onehot(cond):
    return jnp.where(cond, 1.0, 0.0).astype(BF16)


def split2(value):
    hi = value.astype(BF16)
    return hi, (value - hi.astype(F32)).astype(BF16)


def kernel(
    t_ref, w_ref, occ_ref, vir_ref, out_ref, fits_ref,
    q_ref, cols_ref, rows_ref, rt_ref, rbd_ref, tps, tpr, xt, ws, wb, xw, ut, lhs6, msgf, msg, rxa, rxb, rxf,
    ls, rs, spf, spa, spb, rsa, rsb, s2a, s2f, s2b, r2a, r2b, x2s, x2r, dup,
    t_ss, t_rs, w_ss, w_rs, m_ss, m_rs, f_ss, f_rs, a_ss, a_rs, b_ss, b_rs, c_ss, c_rs, d_ss, d_rs, x_ss, x_rs,
):
    amp = lax.axis_index("amp")
    x = lax.axis_index("ctr")
    chip, core = amp // 2, amp % 2
    sib = 1 - core
    y, z = chip // 8, chip % 8

    barrier = pltpu.get_barrier_semaphore()

    @pl.loop(1, NCHIP)
    def _(d):
        q = lax.rem(chip + d, NCHIP)
        pl.semaphore_signal(barrier, inc=1, device_id=(q * 2 + core, x), device_id_type=MESH)

    for d in range(1, 8):
        xx = lax.rem(x + d // 2, NX)
        cc = core if d % 2 == 0 else sib
        pl.semaphore_signal(barrier, inc=1, device_id=(chip * 2 + cc, xx), device_id_type=MESH)

    vrow = jnp.concatenate([vir_ref[r : r + 1, :] for r in range(6)], axis=1)
    occ8 = jnp.broadcast_to(jnp.concatenate([occ_ref[...], jnp.zeros((1, 128 - O), I32)], axis=1), (8, 128))
    occ_i = [occ8[0:1, r : r + 1] for r in range(ITILE)]
    occ_j = [occ8[0:1, ITILE + r : ITILE + r + 1] for r in range(J)]
    own_i = jnp.where(x < 2, jnp.where(x == 0, occ_i[0], occ_i[1]), jnp.where(x == 2, occ_i[2], occ_i[3]))
    own_j = jnp.where(core == 0, occ_j[0], occ_j[1])
    occ_sq = jnp.broadcast_to(occ8[0:1, :], (128, 128))
    occ_cl = occ_sq.T
    r0, r1 = iota((128, 128), 0), iota((128, 128), 1)
    rank_k = jnp.sum(jnp.where((occ_sq == occ_cl) & (r0 < r1) & (r0 < O), 1.0, 0.0), axis=0, keepdims=True)
    picked = onehot(iota((V, 128), 0) == chip * 2 * AB + iota((V, 128), 1))
    vrow8 = jnp.broadcast_to(vrow, (8, V))
    vchip = jnp.dot(vrow8.astype(F32).astype(BF16), picked, preferred_element_type=F32)
    sub8 = iota((8, 128), 0)
    table = jnp.where(
        sub8 == 0,
        occ8.astype(F32),
        jnp.where(sub8 == 1, vchip, jnp.broadcast_to(rank_k, (8, 128))),
    ).astype(BF16)
    lane = iota((1, V), 1)
    deep = iota((128, V), 0)

    def expand(index):
        return jnp.dot(table, onehot(deep == index), preferred_element_type=F32).astype(I32)

    def occ_at(e):
        return e[0:1]

    def vir_at(e):
        return e[1:2]

    def rank_at(e):
        return e[2:3]

    lane_i = lane // (AB * KB)
    lab_i = jnp.where(lane_i < 2, jnp.where(lane_i == 0, occ_i[0], occ_i[1]), jnp.where(lane_i == 2, occ_i[2], occ_i[3]))
    row_t = lab_i ^ occ_at(expand(x * KB + lane % KB)) ^ vir_at(expand(core * AB + (lane % (AB * KB)) // KB))
    e_k = expand(lane % O)
    row_ak = own_i ^ occ_at(e_k) ^ vir_at(expand(core * AB + lane // O))
    e_kc = expand(lane // AB)
    c0 = vir_at(expand(lane % AB))
    c1 = vir_at(expand(AB + lane % AB))
    row_w = occ_at(expand(x * KB + lane // AB)) ^ jnp.where(core == 0, c0, c1)
    chip_c = jnp.where(lane < AB, c0, c1)
    rows_ref[0:1, :] = row_ak
    rows_ref[1:2, :] = occ_at(e_kc) ^ c0 ^ own_j
    rows_ref[2:3, :] = occ_at(e_kc) ^ c1 ^ own_j
    rows_ref[3:4, :] = vrow
    stack = jnp.concatenate([row_t, row_w, rank_at(e_k), rank_at(e_kc), vrow, chip_c, vrow, vrow], axis=0)
    cols_ref[...] = jnp.concatenate([stack] * 16, axis=0).T
    lower = onehot(r0 > r1)
    passed = jnp.zeros((1, 128), F32)
    top = jnp.zeros((1, 1), I32)
    slot = iota((128, 256), 1)
    slot = jnp.where(slot < CAPB, slot, slot - 64)
    for blk in range(6):
        same = jnp.where(cols_ref[blk * 128 : (blk + 1) * 128, 4:5] == r1, 1.0, 0.0)
        counts = jnp.dot(lower, same.astype(BF16), preferred_element_type=F32) + passed
        rank = jnp.sum(counts * same, axis=1, keepdims=True).astype(I32)
        passed = passed + jnp.sum(same, axis=0, keepdims=True)
        q_ref[blk * 128 : (blk + 1) * 128, :] = onehot(rank == slot)
    low = jnp.max(passed, axis=1, keepdims=True) <= CAPB
    fits = low & (jnp.max(jnp.where(r1[0:1, :] < O, rank_k, 0.0), axis=1, keepdims=True) < CAPK)
    fits_ref[...] = jnp.broadcast_to(jnp.where(fits, 1, 0), (8, 128))

    left = iota((1, 128), 1) < 64
    half0, half1 = onehot(left), onehot(jnp.logical_not(left))

    def pair_up(first, second):
        return jnp.where(left, first, second)

    def t_copy(xx, slot):
        return pltpu.make_async_remote_copy(
            src_ref=tps.at[xx], dst_ref=tpr.at[:, slot], send_sem=t_ss.at[xx], recv_sem=t_rs.at[slot],
            device_id=(amp, xx), device_id_type=MESH,
        )

    for d in (1, 2, 3, 4):
        i = lax.rem(x + d, NX)
        rows = pl.ds(pl.multiple_of(i * AB * KB, AB * KB), AB * KB)
        keep = cols_ref[rows, 0:1] == rows_ref[3:4, :]
        masked = jnp.where(keep, t_ref[rows, :].astype(F32), 0.0).astype(BF16)
        packed = jnp.dot(masked, q_ref[...], preferred_element_type=F32)
        tps[i, 0:AB] = packed[:, 0:128].astype(BF16).reshape(AB, KB, 128)
        half = AB * KB // 2
        tps[i, AB:] = pair_up(packed[0:half, 128:], packed[half:, 128:]).astype(BF16).reshape(AB // 2, KB, 128)
        if d == 1:
            pl.semaphore_wait(barrier, NCHIP - 1 + 7)
        if d < 4:
            t_copy(i, x).start()
    tpr[:, x] = tps[x]

    for j in range(J):
        keep = (cols_ref[0 : KB * AB, 1:2] ^ occ_j[j]) == rows_ref[3:4, :]
        masked = jnp.where(keep, w_ref[j].astype(F32), 0.0).astype(BF16)
        packed = jnp.dot(masked, q_ref[...], preferred_element_type=F32)
        half = AB * KB // 2
        ws[j, 0 : 2 * half] = packed[:, 0:128].astype(BF16)
        ws[j, 2 * half :] = pair_up(packed[0:half, 128:], packed[half:, 128:]).astype(BF16)

    def w_copy(xx, cc, slot_x, slot_c):
        return pltpu.make_async_remote_copy(
            src_ref=ws.at[cc], dst_ref=wb.at[slot_c, slot_x], send_sem=w_ss.at[cc, xx], recv_sem=w_rs.at[slot_c, slot_x],
            device_id=(chip * 2 + cc, xx), device_id_type=MESH,
        )

    for d in range(1, 8):
        w_copy(lax.rem(x + d // 2, NX), core if d % 2 == 0 else sib, x, core).start()
    wb[core, x] = ws[core]

    pair = iota((V, 256), 1)
    inner = pair % 128
    deep_t = iota((V, 256), 0)
    rt_ref[...] = onehot(
        (inner // CAPK == deep_t // 128)
        & (pair // 128 == (deep_t % 128) // O)
        & (inner % CAPK == cols_ref[:, 2:3])
        & (inner < 6 * CAPK)
    )
    rbd_ref[...] = onehot(
        ((pair // 128) * 6 + inner // CAPK == deep_t % AB)
        & (inner % CAPK == cols_ref[:, 3:4])
        & (inner < 6 * CAPK)
    )

    for d in range(1, NX):
        xx = lax.rem(x + d, NX)
        t_copy(xx, xx).wait_recv()

    xt[:, 0:128] = tpr[0:AB].reshape(V, 128)
    both = tpr[AB:].reshape(V // 2, 128)
    xt[0 : V // 2, 128:] = both * half0
    xt[V // 2 :, 128:] = both * half1

    def m_copy(q, slot):
        return pltpu.make_async_remote_copy(
            src_ref=msg.at[q], dst_ref=rxa.at[slot], send_sem=m_ss.at[q], recv_sem=m_rs.at[slot],
            device_id=(q * 2 + core, x), device_id_type=MESH,
        )

    def f_copy(q):
        return pltpu.make_async_remote_copy(
            src_ref=rxa.at[q], dst_ref=rxb.at[q], send_sem=f_ss.at[q], recv_sem=f_rs.at[q],
            device_id=(chip * 2 + sib, x), device_id_type=MESH,
        )

    HC = NCHIP // 2

    @pl.loop(0, 2)
    def _(hh):
        h = lax.rem(chip // HC + 1 + hh, 2)
        rows = pl.ds(pl.multiple_of(h * (V // 2), V // 2), V // 2)
        full = lax.dot_general(q_ref[rows, :], xt[...], NT, preferred_element_type=F32)
        full = jnp.where(cols_ref[rows, 4:5] == rows_ref[0:1, :], full, 0.0)
        for t in range(6):
            ut[t] = full[:, t * 128 : (t + 1) * 128]

        @pl.loop(0, 4)
        def _(g):
            for t in range(6):
                for c6 in range(6):
                    piece = ut[t, pl.ds(g * 6 + c6, HC, stride=24), :]
                    lhs6[t * HC : (t + 1) * HC, c6 * 128 : (c6 + 1) * 128] = piece.astype(BF16)
            packed = jnp.dot(lhs6[...], rt_ref[...], preferred_element_type=F32)
            for t in range(6):
                for a2 in range(2):
                    msgf[pl.ds((2 * t + a2) * 4 + g, HC, stride=48), :] = packed[
                        t * HC : (t + 1) * HC, a2 * 128 : (a2 + 1) * 128
                    ]

        msg[pl.ds(h * HC, HC)] = msgf[...].astype(BF16).reshape(HC, 48, 128)

        @pl.loop(0, HC)
        def _(d):
            q = h * HC + lax.rem(chip + 1 + d, HC)

            @pl.when(q != chip)
            def _():
                m_copy(q, chip).start()

    rxa[chip] = msg[chip]
    f_copy(chip).start()

    for d in range(1, 8):
        xx, cc = lax.rem(x + d // 2, NX), core if d % 2 == 0 else sib
        w_copy(xx, cc, xx, cc).wait_recv()
    for c in range(2):
        for xx in range(NX):
            base = xx * AB * KB
            half = AB * KB // 2
            xw[c, base : base + 2 * half, 0:128] = wb[c, xx, 0 : 2 * half]
            xw[c, base : base + half, 128:] = wb[c, xx, 2 * half :] * half0
            xw[c, base + half : base + 2 * half, 128:] = wb[c, xx, 2 * half :] * half1

    @pl.loop(0, 3)
    def _(m):
        rows = pl.ds(pl.multiple_of(m * 256, 256), 256)
        for c in range(2):
            full = lax.dot_general(q_ref[rows, :], xw[c], NT, preferred_element_type=F32)
            full = jnp.where(cols_ref[rows, 4:5] == rows_ref[1 + c : 2 + c, :], full, 0.0).astype(BF16)
            packed = jnp.dot(full, rbd_ref[...], preferred_element_type=F32).astype(BF16)
            ls[rows, 512 + c * 256 : 768 + c * 256] = packed
            rs[rows, c * 256 : (c + 1) * 256] = packed

    rxf[pl.ds(pl.multiple_of((chip * 2 + core) * 48, 48), 48), :] = rxa[chip].astype(F32)

    @pl.loop(0, 2)
    def _(hh):
        h = lax.rem(chip // HC + 1 + hh, 2)

        @pl.loop(0, HC)
        def _(d):
            q = h * HC + lax.rem(chip + 2 * HC - 1 - d, HC)

            @pl.when(q != chip)
            def _():
                m_copy(q, q).wait_recv()
                f_copy(q).start()
                rxf[pl.ds(pl.multiple_of((q * 2 + core) * 48, 48), 48), :] = rxa[q].astype(F32)

    @pl.loop(0, NCHIP)
    def _(d):
        q = lax.rem(chip + d, NCHIP)
        f_copy(q).wait_recv()
        rxf[pl.ds(pl.multiple_of((q * 2 + sib) * 48, 48), 48), :] = rxb[q].astype(F32)

    for g in range(4):
        piece = rxf[pl.ds(g, V, stride=4), :].astype(BF16)
        ls[:, g * 128 : (g + 1) * 128] = piece
        rs[:, 512 + g * 128 : 640 + g * 128] = piece

    def a_copy(yy, slot):
        return pltpu.make_async_remote_copy(
            src_ref=spa.at[yy], dst_ref=rsa.at[slot], send_sem=a_ss.at[yy], recv_sem=a_rs.at[slot],
            device_id=((yy * 8 + z) * 2 + core, x), device_id_type=MESH,
        )

    def b_copy(zz, slot):
        return pltpu.make_async_remote_copy(
            src_ref=spb.at[pl.ds(pl.multiple_of(zz * 48, 48), 48)], dst_ref=rsb.at[slot],
            send_sem=b_ss.at[zz], recv_sem=b_rs.at[slot],
            device_id=((y * 8 + zz) * 2 + core, x), device_id_type=MESH,
        )

    def c_copy(zz, slot):
        return pltpu.make_async_remote_copy(
            src_ref=s2a.at[zz], dst_ref=r2a.at[slot], send_sem=c_ss.at[zz], recv_sem=c_rs.at[slot],
            device_id=((y * 8 + zz) * 2 + core, x), device_id_type=MESH,
        )

    def d_copy(yy, slot):
        return pltpu.make_async_remote_copy(
            src_ref=s2b.at[yy], dst_ref=r2b.at[slot], send_sem=d_ss.at[yy], recv_sem=d_rs.at[slot],
            device_id=((yy * 8 + z) * 2 + core, x), device_id_type=MESH,
        )

    for step in range(1, 5):
        yy = lax.rem(y + step, 4)
        rows = pl.ds(pl.multiple_of(yy * 192, 192), 192)
        full = lax.dot_general(ls[rows, :], rs[...], NT, preferred_element_type=F32)
        keep = cols_ref[rows, 4:5] == (rows_ref[3:4, :] ^ (own_i ^ own_j))
        hi, lo = split2(jnp.where(keep, full, 0.0))
        packed = jnp.dot(hi, q_ref[...], preferred_element_type=F32)
        packed += jnp.dot(lo, q_ref[...], preferred_element_type=F32)
        spa[yy] = packed[:, 0:128]
        if step < 4:
            a_copy(yy, y).start()
        spf[...] = packed[:, 128:]
        spb[pl.ds(yy, 96, stride=4), :] = pair_up(spf[pl.ds(0, 96, stride=2), :], spf[pl.ds(1, 96, stride=2), :])

    for d in range(1, 8):
        b_copy(lax.rem(z + d, 8), z).start()
    rsa[y] = spa[y]
    rsb[z] = spb[pl.ds(pl.multiple_of(z * 48, 48), 48), :]
    for d in range(1, 4):
        yy = lax.rem(y + d, 4)
        a_copy(yy, yy).wait_recv()
    s2a[...] = jnp.sum(rsa[...], axis=0).reshape(8, 24, 128)
    for d in range(1, 8):
        c_copy(lax.rem(z + d, 8), z).start()
    r2a[z] = s2a[z]
    for d in range(1, 8):
        zz = lax.rem(z + d, 8)
        b_copy(zz, zz).wait_recv()
    s2f[...] = jnp.sum(rsb[...], axis=0)
    for yy in range(4):
        s2b[yy] = jnp.concatenate([s2f[pl.ds(yy, 12, stride=4), :], jnp.zeros((4, 128), F32)], axis=0)
    for d in range(1, 4):
        d_copy(lax.rem(y + d, 4), y).start()
    r2b[y] = s2b[y]
    for d in range(1, 8):
        zz = lax.rem(z + d, 8)
        c_copy(zz, zz).wait_recv()
    for d in range(1, 4):
        yy = lax.rem(y + d, 4)
        d_copy(yy, yy).wait_recv()

    x2s[0:24, :] = jnp.sum(r2a[...], axis=0)
    x2s[24:40, :] = jnp.sum(r2b[...], axis=0)
    swap = pltpu.make_async_remote_copy(
        src_ref=x2s, dst_ref=x2r, send_sem=x_ss, recv_sem=x_rs, device_id=(chip * 2 + sib, x), device_id_type=MESH
    )
    swap.start()
    swap.wait_recv()
    for j in range(J):
        own = jnp.where(core == j, x2s[...], x2r[...])
        tail = own[24:36]
        dup[j, pl.ds(0, AB, stride=2), :] = jnp.where(left, tail, 0.0)
        dup[j, pl.ds(1, AB, stride=2), :] = jnp.where(left, 0.0, tail)
        hi, lo = split2(jnp.concatenate([own[0:24], dup[j]], axis=1))
        full = lax.dot_general(hi, q_ref[...], NT, preferred_element_type=F32)
        full += lax.dot_general(lo, q_ref[...], NT, preferred_element_type=F32)
        keep = cols_ref[0:24, 5:6] == (rows_ref[3:4, :] ^ (own_i ^ occ_j[j]))
        full = jnp.where(keep, full, 0.0)
        out_ref[:, j, :] = jnp.where(core == 0, full[0:AB], full[AB:])

    for d in range(1, NX):
        t_copy(lax.rem(x + d, NX), x).wait_send()
        a_copy(lax.rem(y + d, 4), y).wait_send()
        d_copy(lax.rem(y + d, 4), y).wait_send()
    for d in range(1, 8):
        w_copy(lax.rem(x + d // 2, NX), core if d % 2 == 0 else sib, x, core).wait_send()
        b_copy(lax.rem(z + d, 8), z).wait_send()
        c_copy(lax.rem(z + d, 8), z).wait_send()
    swap.wait_send()
    f_copy(chip).wait_send()

    @pl.loop(1, NCHIP)
    def _(d):
        q = lax.rem(chip + d, NCHIP)
        m_copy(q, chip).wait_send()
        f_copy(q).wait_send()


def packed_shards(amplitudes, integrals, occ_irrep, vir_irrep):
    t = amplitudes.reshape(ITILE * AB * KB, V)
    w = jnp.transpose(integrals, (2, 0, 1, 3)).reshape(J, KB * AB, V)
    vm = pltpu.VMEM
    dma = pltpu.SemaphoreType.DMA
    out, fits = pl.pallas_call(
        kernel,
        out_shape=(jax.ShapeDtypeStruct((AB, J, V), F32), jax.ShapeDtypeStruct((8, 128), I32)),
        in_specs=[pl.BlockSpec(memory_space=vm)] * 4,
        out_specs=(pl.BlockSpec(memory_space=vm),) * 2,
        scratch_shapes=[
            vm((V, 256), BF16), vm((V, 128), I32), vm((8, V), I32), vm((V, 256), BF16), vm((V, 256), BF16),
            vm((ITILE, AB * 3 // 2, KB, 128), BF16), vm((AB * 3 // 2, NX, KB, 128), BF16), vm((V, 256), BF16),
            vm((J, KB * AB * 3 // 2, 128), BF16), vm((2, NX, KB * AB * 3 // 2, 128), BF16), vm((2, V, 256), BF16),
            vm((6, V // 2, 128), F32), vm((3 * NCHIP, V), BF16), vm((NCHIP * 24, 128), F32),
            vm((NCHIP, 48, 128), BF16), vm((NCHIP, 48, 128), BF16), vm((NCHIP, 48, 128), BF16),
            vm((2 * NCHIP * 48, 128), F32),
            vm((V, 1024), BF16), vm((V, 1024), BF16),
            vm((192, 128), F32), vm((4, 192, 128), F32), vm((8 * 48, 128), F32), vm((4, 192, 128), F32), vm((8, 48, 128), F32),
            vm((8, 24, 128), F32), vm((48, 128), F32), vm((4, 16, 128), F32), vm((8, 24, 128), F32), vm((4, 16, 128), F32),
            vm((40, 128), F32), vm((40, 128), F32), vm((J, 24, 128), F32),
            dma((NX,)), dma((NX,)), dma((2, NX)), dma((2, NX)), dma((NCHIP,)), dma((NCHIP,)), dma((NCHIP,)), dma((NCHIP,)),
            dma((4,)), dma((4,)), dma((8,)), dma((8,)), dma((8,)), dma((8,)), dma((4,)), dma((4,)), dma, dma,
        ],
        compiler_params=pltpu.CompilerParams(
            collective_id=0, has_side_effects=True, vmem_limit_bytes=48 * 1024 * 1024
        ),
        cost_estimate=pl.CostEstimate(flops=6_000_000_000, bytes_accessed=4_000_000, transcendentals=0),
    )(t, w, occ_irrep.reshape(1, O), vir_irrep.reshape(6, 128))
    return out[None], fits[0, 0]


def shards(amplitudes, integrals, occ_irrep, vir_irrep):
    packed, fits = packed_shards(amplitudes, integrals, occ_irrep, vir_irrep)
    return lax.cond(
        fits > 0,
        lambda *args: packed,
        dense_shards,
        amplitudes,
        integrals,
        occ_irrep,
        vir_irrep,
    )


def solution(mesh):
    return jax.shard_map(
        shards,
        mesh=mesh,
        in_specs=(P(None, "amp", "ctr", None), P("ctr", "amp", None, None), P(), P()),
        out_specs=P("ctr", "amp", None, None),
        check_vma=False,
    )
```

```python
import functools

import jax
import jax.numpy as jnp
from jax import lax
from jax.experimental import pallas as pl
from jax.experimental.pallas import tpu as pltpu
from jax.sharding import PartitionSpec as P

O, V, ITILE, J = 64, 768, 4, 2
NX, NCHIP, AB = 4, 32, 12
KB = O // NX
CAPB = 192
CAPK = 21
MESH = pl.DeviceIdType.MESH
F32, BF16, I32 = jnp.float32, jnp.bfloat16, jnp.int32
NT = (((1,), (1,)), ((), ()))


def dense_shards(amplitudes, integrals, occ_irrep, vir_irrep):
    regrouped = lax.all_to_all(
        lax.all_to_all(amplitudes, "amp", split_axis=3, concat_axis=1, tiled=True),
        "ctr",
        split_axis=0,
        concat_axis=2,
        tiled=True,
    )
    own_rows, vir_full, occ_full, vir_local = regrouped.shape
    tile_size = own_rows * lax.axis_size("ctr")
    pair_count = integrals.shape[2]
    vir_block = lax.dynamic_slice_in_dim(vir_irrep, lax.axis_index("amp") * vir_local, vir_local)
    occ_tile = lax.dynamic_slice_in_dim(occ_irrep, lax.axis_index("ctr") * own_rows, own_rows)
    pair_labels = lax.dynamic_slice_in_dim(occ_irrep, tile_size, pair_count)
    t_left = jnp.bitwise_xor(occ_tile[:, None, None, None], vir_irrep[None, :, None, None])
    t_right = jnp.bitwise_xor(occ_irrep[None, None, :, None], vir_block[None, None, None, :])
    masked_amps = jnp.where(t_left == t_right, regrouped, jnp.zeros_like(regrouped))
    amp_matrix = masked_amps.reshape(own_rows * vir_full, occ_full * vir_local)
    w_right = jnp.bitwise_xor(pair_labels[None, None, :, None], vir_irrep[None, None, None, :])
    copies = jnp.broadcast_to(integrals[None], (lax.axis_size("ctr"),) + integrals.shape)
    integral_block = lax.all_to_all(copies, "ctr", split_axis=0, concat_axis=0, tiled=True)
    integral_block = integral_block.reshape((-1,) + integrals.shape[1:])
    count = integral_block.shape[0]
    w_left = jnp.bitwise_xor(occ_irrep[:, None, None, None], vir_block[None, :, None, None])
    w_masked = jnp.where(w_left == w_right, integral_block, jnp.zeros_like(integral_block))
    w_matrix = w_masked.reshape(count * vir_local, pair_count * vir_full)
    partial_value = jnp.dot(amp_matrix, w_matrix, preferred_element_type=jnp.float32)
    partial_value = partial_value.reshape(own_rows, vir_full, pair_count, vir_full)
    pieces = partial_value.reshape(lax.axis_size("amp"), own_rows, vir_local, pair_count, vir_full)
    summed = jnp.sum(lax.all_to_all(pieces, "amp", split_axis=0, concat_axis=0, tiled=True), axis=0)
    swapped = lax.all_to_all(summed, "amp", split_axis=3, concat_axis=1, tiled=True)
    return summed + jnp.transpose(swapped, (0, 3, 2, 1))


def iota(shape, dim):
    return lax.broadcasted_iota(I32, shape, dim)


def onehot(cond):
    return jnp.where(cond, 1.0, 0.0).astype(BF16)


def split2(value):
    hi = value.astype(BF16)
    return hi, (value - hi.astype(F32)).astype(BF16)


def drain(ref, sem):
    pltpu.make_async_copy(ref, ref, sem).wait()


def kernel(
    t_ref, w_ref, occ_ref, vir_ref, out_ref, fits_ref,
    tv, wv, q_ref, cols_ref, cols2_ref, rows_ref, rt_ref, rbd_ref, tps, tpr, xt, ws, wb, xw, ut, lhs6, msgf, msg, rxa, rxb, rxf,
    ls, rs, spf, spa, spb, rsa, rsb, s2a, s2f, s2b, r2a, r2b, x2s, x2r, dup,
    tv_s, wv_s,
    t_ss, t_rs, w_ss, w_rs, m_ss, m_rs, f_ss, f_rs, a_ss, a_rs, b_ss, b_rs, c_ss, c_rs, d_ss, d_rs, x_ss, x_rs,
):
    amp = lax.axis_index("amp")
    x = lax.axis_index("ctr")
    chip, core = amp // 2, amp % 2
    sib = 1 - core
    y, z = chip // 8, chip % 8

    t_in = pltpu.make_async_copy(t_ref, tv, tv_s)
    w_in = pltpu.make_async_copy(w_ref, wv, wv_s)
    t_in.start()
    w_in.start()
    barrier = pltpu.get_barrier_semaphore()

    @pl.loop(1, NCHIP)
    def _(d):
        q = lax.rem(chip + d, NCHIP)
        pl.semaphore_signal(barrier, inc=1, device_id=(q * 2 + core, x), device_id_type=MESH)

    for d in range(1, 8):
        xx = lax.rem(x + d // 2, NX)
        cc = core if d % 2 == 0 else sib
        pl.semaphore_signal(barrier, inc=1, device_id=(chip * 2 + cc, xx), device_id_type=MESH)

    vrow = jnp.concatenate([vir_ref[r : r + 1, :] for r in range(6)], axis=1)
    occ8 = jnp.broadcast_to(jnp.concatenate([occ_ref[...], jnp.zeros((1, 128 - O), I32)], axis=1), (8, 128))
    occ_i = [occ8[0:1, r : r + 1] for r in range(ITILE)]
    occ_j = [occ8[0:1, ITILE + r : ITILE + r + 1] for r in range(J)]
    own_i = jnp.where(x < 2, jnp.where(x == 0, occ_i[0], occ_i[1]), jnp.where(x == 2, occ_i[2], occ_i[3]))
    own_j = jnp.where(core == 0, occ_j[0], occ_j[1])
    occ_sq = jnp.broadcast_to(occ8[0:1, :], (128, 128))
    occ_cl = occ_sq.T
    r0, r1 = iota((128, 128), 0), iota((128, 128), 1)
    rank_k = jnp.sum(jnp.where((occ_sq == occ_cl) & (r0 < r1) & (r0 < O), 1.0, 0.0), axis=0, keepdims=True)
    picked = onehot(iota((V, 128), 0) == chip * 2 * AB + iota((V, 128), 1))
    vrow8 = jnp.broadcast_to(vrow, (8, V))
    vchip = jnp.dot(vrow8.astype(F32).astype(BF16), picked, preferred_element_type=F32)
    sub8 = iota((8, 128), 0)
    table = jnp.where(
        sub8 == 0,
        occ8.astype(F32),
        jnp.where(sub8 == 1, vchip, jnp.broadcast_to(rank_k, (8, 128))),
    ).astype(BF16)
    lane = iota((1, V), 1)
    deep = iota((128, V), 0)

    def expand(index):
        return jnp.dot(table, onehot(deep == index), preferred_element_type=F32).astype(I32)

    def occ_at(e):
        return e[0:1]

    def vir_at(e):
        return e[1:2]

    def rank_at(e):
        return e[2:3]

    lane_i = lane // (AB * KB)
    lab_i = jnp.where(lane_i < 2, jnp.where(lane_i == 0, occ_i[0], occ_i[1]), jnp.where(lane_i == 2, occ_i[2], occ_i[3]))
    row_t = lab_i ^ occ_at(expand(x * KB + lane % KB)) ^ vir_at(expand(core * AB + (lane % (AB * KB)) // KB))
    rows_ref[3:4, :] = vrow
    cols_ref[...] = jnp.concatenate([jnp.concatenate([row_t, vrow, vrow, vrow], axis=0)] * 32, axis=0).T
    lower = onehot(r0 > r1)
    passed = jnp.zeros((1, 128), F32)
    top = jnp.zeros((1, 1), I32)
    slot = iota((128, 256), 1)
    slot = jnp.where(slot < CAPB, slot, slot - 64)
    for blk in range(6):
        same = jnp.where(cols_ref[blk * 128 : (blk + 1) * 128, 1:2] == r1, 1.0, 0.0)
        counts = jnp.dot(lower, same.astype(BF16), preferred_element_type=F32) + passed
        rank = jnp.sum(counts * same, axis=1, keepdims=True).astype(I32)
        passed = passed + jnp.sum(same, axis=0, keepdims=True)
        q_ref[blk * 128 : (blk + 1) * 128, :] = onehot(rank == slot)
    low = jnp.max(passed, axis=1, keepdims=True) <= CAPB
    fits = low & (jnp.max(jnp.where(r1[0:1, :] < O, rank_k, 0.0), axis=1, keepdims=True) < CAPK)
    fits_ref[0, 0] = jnp.max(jnp.where(fits, 1.0, 0.0))

    left = iota((1, 128), 1) < 64
    half0, half1 = onehot(left), onehot(jnp.logical_not(left))

    def pair_up(first, second):
        return jnp.where(left, first, second)

    def t_copy(e, xx, slot):
        return pltpu.make_async_remote_copy(
            src_ref=tps.at[e, xx], dst_ref=tpr.at[e, :, slot], send_sem=t_ss, recv_sem=t_rs.at[e],
            device_id=(amp, xx), device_id_type=MESH,
        )

    t_in.wait()
    GR = 4 * KB
    for e in range(3):
        pieces = []
        for i in range(ITILE):
            start = i * AB * KB + e * GR
            keep = cols_ref[start : start + GR, 0:1] == rows_ref[3:4, :]
            pieces.append(jnp.where(keep, tv[start : start + GR, :].astype(F32), 0.0).astype(BF16))
        packed = jnp.dot(jnp.concatenate(pieces, axis=0), q_ref[...], preferred_element_type=F32)
        for i in range(ITILE):
            start = i * GR
            tps[e, i, 0:4] = packed[start : start + GR, 0:128].astype(BF16).reshape(4, KB, 128)
            tail = pair_up(packed[start : start + GR // 2, 128:], packed[start + GR // 2 : start + GR, 128:])
            tps[e, i, 4:] = tail.astype(BF16).reshape(2, KB, 128)
        if e == 0:
            pl.semaphore_wait(barrier, NCHIP - 1 + 7)
        for d in range(1, NX):
            t_copy(e, lax.rem(x + d, NX), x).start()
        tpr[e, :, x] = tps[e, x]

    e_k = expand(lane % O)
    row_ak = own_i ^ occ_at(e_k) ^ vir_at(expand(core * AB + lane // O))
    e_kc = expand(lane // AB)
    c0 = vir_at(expand(lane % AB))
    c1 = vir_at(expand(AB + lane % AB))
    row_w = occ_at(expand(x * KB + lane // AB)) ^ jnp.where(core == 0, c0, c1)
    chip_c = jnp.where(lane < AB, c0, c1)
    rows_ref[0:1, :] = row_ak
    rows_ref[1:2, :] = occ_at(e_kc) ^ c0 ^ own_j
    rows_ref[2:3, :] = occ_at(e_kc) ^ c1 ^ own_j
    stack = jnp.concatenate([row_w, rank_at(e_k), rank_at(e_kc), chip_c], axis=0)
    cols2_ref[...] = jnp.concatenate([stack] * 32, axis=0).T

    w_in.wait()
    for j in range(J):
        keep = (cols2_ref[0 : KB * AB, 0:1] ^ occ_j[j]) == rows_ref[3:4, :]
        masked = jnp.where(keep, wv[:, j, :].astype(F32), 0.0).astype(BF16)
        packed = jnp.dot(masked, q_ref[...], preferred_element_type=F32)
        half = AB * KB // 2
        ws[j, 0 : 2 * half] = packed[:, 0:128].astype(BF16)
        ws[j, 2 * half :] = pair_up(packed[0:half, 128:], packed[half:, 128:]).astype(BF16)

    def w_copy(xx, cc, slot_x, slot_c):
        return pltpu.make_async_remote_copy(
            src_ref=ws.at[cc], dst_ref=wb.at[slot_c * NX + slot_x], send_sem=w_ss, recv_sem=w_rs,
            device_id=(chip * 2 + cc, xx), device_id_type=MESH,
        )

    for d in range(1, 8):
        w_copy(lax.rem(x + d // 2, NX), core if d % 2 == 0 else sib, x, core).start()
    wb[core * NX + x] = ws[core]

    pair = iota((V, 256), 1)
    inner = pair % 128
    deep_t = iota((V, 256), 0)
    rt_ref[...] = onehot(
        (inner // CAPK == deep_t // 128)
        & (pair // 128 == (deep_t % 128) // O)
        & (inner % CAPK == cols2_ref[:, 1:2])
        & (inner < 6 * CAPK)
    )
    rbd_ref[...] = onehot(
        ((pair // 128) * 6 + inner // CAPK == deep_t % AB)
        & (inner % CAPK == cols2_ref[:, 2:3])
        & (inner < 6 * CAPK)
    )

    def m_copy(e, q, slot):
        return pltpu.make_async_remote_copy(
            src_ref=msg.at[e, q], dst_ref=rxa.at[e, slot], send_sem=m_ss, recv_sem=m_rs.at[e],
            device_id=(q * 2 + core, x), device_id_type=MESH,
        )

    def f_copy(e):
        return pltpu.make_async_remote_copy(
            src_ref=rxa.at[e], dst_ref=rxb.at[e], send_sem=f_ss, recv_sem=f_rs.at[e],
            device_id=(chip * 2 + sib, x), device_id_type=MESH,
        )

    for e in range(3):
        drain(tpr.at[e, :, 0:3], t_rs.at[e])
        xt[:, 0:128] = tpr[e, 0:4].reshape(4 * O, 128)
        both = tpr[e, 4:].reshape(2 * O, 128)
        xt[0 : 2 * O, 128:] = both * half0
        xt[2 * O :, 128:] = both * half1
        full = lax.dot_general(q_ref[...], xt[...], NT, preferred_element_type=F32)
        full = jnp.where(cols_ref[:, 1:2] == rows_ref[0:1, e * 256 : (e + 1) * 256], full, 0.0)
        for t in range(2):
            ut[t] = full[:, t * 128 : (t + 1) * 128]
        for g in range(4):
            for t in range(2):
                for c6 in range(6):
                    piece = ut[t, pl.ds(g * 6 + c6, NCHIP, stride=24), :]
                    base = (g * 2 + t) * NCHIP
                    lhs6[base : base + NCHIP, c6 * 128 : (c6 + 1) * 128] = piece.astype(BF16)
        packed = jnp.dot(lhs6[...], rt_ref[...], preferred_element_type=F32)
        for g in range(4):
            for t in range(2):
                for a2 in range(2):
                    base = (g * 2 + t) * NCHIP
                    msgf[pl.ds((2 * t + a2) * 4 + g, NCHIP, stride=16), :] = packed[
                        base : base + NCHIP, a2 * 128 : (a2 + 1) * 128
                    ]
        msg[e] = msgf[...].astype(BF16).reshape(NCHIP, 16, 128)

        @pl.loop(1, NCHIP)
        def _(d):
            m_copy(e, lax.rem(chip + d, NCHIP), chip).start()

        rxa[e, chip] = msg[e, chip]

    drain(wb.at[0:7], w_rs)
    for c in range(2):
        for xx in range(NX):
            base = xx * AB * KB
            half = AB * KB // 2
            xw[c, base : base + 2 * half, 0:128] = wb[c * NX + xx, 0 : 2 * half]
            xw[c, base : base + half, 128:] = wb[c * NX + xx, 2 * half :] * half0
            xw[c, base + half : base + 2 * half, 128:] = wb[c * NX + xx, 2 * half :] * half1

    @pl.loop(0, 3)
    def _(m):
        rows = pl.ds(pl.multiple_of(m * 256, 256), 256)
        for c in range(2):
            full = lax.dot_general(q_ref[rows, :], xw[c], NT, preferred_element_type=F32)
            full = jnp.where(cols_ref[rows, 1:2] == rows_ref[1 + c : 2 + c, :], full, 0.0).astype(BF16)
            packed = jnp.dot(full, rbd_ref[...], preferred_element_type=F32).astype(BF16)
            ls[rows, 512 + c * 256 : 768 + c * 256] = packed
            rs[rows, c * 256 : (c + 1) * 256] = packed

    for e in range(3):
        drain(rxa.at[e, 0 : NCHIP - 1], m_rs.at[e])
        f_copy(e).start()

        @pl.loop(0, NCHIP)
        def _(q):
            rxf[pl.ds(pl.multiple_of((q * 2 + core) * 48 + e * 16, 16), 16), :] = rxa[e, q].astype(F32)

    for e in range(3):
        drain(rxb.at[e], f_rs.at[e])

        @pl.loop(0, NCHIP)
        def _(q):
            rxf[pl.ds(pl.multiple_of((q * 2 + sib) * 48 + e * 16, 16), 16), :] = rxb[e, q].astype(F32)

    for g in range(4):
        piece = rxf[pl.ds(g, V, stride=4), :].astype(BF16)
        ls[:, g * 128 : (g + 1) * 128] = piece
        rs[:, 512 + g * 128 : 640 + g * 128] = piece

    def a_copy(yy, slot):
        return pltpu.make_async_remote_copy(
            src_ref=spa.at[yy], dst_ref=rsa.at[slot], send_sem=a_ss, recv_sem=a_rs,
            device_id=((yy * 8 + z) * 2 + core, x), device_id_type=MESH,
        )

    def b_copy(zz, slot):
        return pltpu.make_async_remote_copy(
            src_ref=spb.at[pl.ds(pl.multiple_of(zz * 48, 48), 48)], dst_ref=rsb.at[slot],
            send_sem=b_ss, recv_sem=b_rs,
            device_id=((y * 8 + zz) * 2 + core, x), device_id_type=MESH,
        )

    def c_copy(zz, slot):
        return pltpu.make_async_remote_copy(
            src_ref=s2a.at[zz], dst_ref=r2a.at[slot], send_sem=c_ss, recv_sem=c_rs,
            device_id=((y * 8 + zz) * 2 + core, x), device_id_type=MESH,
        )

    def d_copy(yy, slot):
        return pltpu.make_async_remote_copy(
            src_ref=s2b.at[yy], dst_ref=r2b.at[slot], send_sem=d_ss, recv_sem=d_rs,
            device_id=((yy * 8 + z) * 2 + core, x), device_id_type=MESH,
        )

    for step in range(1, 5):
        yy = lax.rem(y + step, 4)
        rows = pl.ds(pl.multiple_of(yy * 192, 192), 192)
        full = lax.dot_general(ls[rows, :], rs[...], NT, preferred_element_type=F32)
        keep = cols_ref[rows, 1:2] == (rows_ref[3:4, :] ^ (own_i ^ own_j))
        hi, lo = split2(jnp.where(keep, full, 0.0))
        packed = jnp.dot(hi, q_ref[...], preferred_element_type=F32)
        packed += jnp.dot(lo, q_ref[...], preferred_element_type=F32)
        spa[yy] = packed[:, 0:128]
        if step < 4:
            a_copy(yy, y).start()
        spf[...] = packed[:, 128:]
        spb[pl.ds(yy, 96, stride=4), :] = pair_up(spf[pl.ds(0, 96, stride=2), :], spf[pl.ds(1, 96, stride=2), :])

    for d in range(1, 8):
        b_copy(lax.rem(z + d, 8), z).start()
    rsa[y] = spa[y]
    rsb[z] = spb[pl.ds(pl.multiple_of(z * 48, 48), 48), :]
    drain(rsa.at[0:3], a_rs)
    s2a[...] = jnp.sum(rsa[...], axis=0).reshape(8, 24, 128)
    for d in range(1, 8):
        c_copy(lax.rem(z + d, 8), z).start()
    r2a[z] = s2a[z]
    drain(rsb.at[0:7], b_rs)
    s2f[...] = jnp.sum(rsb[...], axis=0)
    for yy in range(4):
        s2b[yy] = jnp.concatenate([s2f[pl.ds(yy, 12, stride=4), :], jnp.zeros((4, 128), F32)], axis=0)
    for d in range(1, 4):
        d_copy(lax.rem(y + d, 4), y).start()
    r2b[y] = s2b[y]
    drain(r2a.at[0:7], c_rs)
    drain(r2b.at[0:3], d_rs)

    x2s[0:24, :] = jnp.sum(r2a[...], axis=0)
    x2s[24:40, :] = jnp.sum(r2b[...], axis=0)
    swap = pltpu.make_async_remote_copy(
        src_ref=x2s, dst_ref=x2r, send_sem=x_ss, recv_sem=x_rs, device_id=(chip * 2 + sib, x), device_id_type=MESH
    )
    swap.start()
    swap.wait_recv()
    for j in range(J):
        own = jnp.where(core == j, x2s[...], x2r[...])
        tail = own[24:36]
        dup[j, pl.ds(0, AB, stride=2), :] = jnp.where(left, tail, 0.0)
        dup[j, pl.ds(1, AB, stride=2), :] = jnp.where(left, 0.0, tail)
        hi, lo = split2(jnp.concatenate([own[0:24], dup[j]], axis=1))
        full = lax.dot_general(hi, q_ref[...], NT, preferred_element_type=F32)
        full += lax.dot_general(lo, q_ref[...], NT, preferred_element_type=F32)
        keep = cols2_ref[0:24, 3:4] == (rows_ref[3:4, :] ^ (own_i ^ occ_j[j]))
        full = jnp.where(keep, full, 0.0)
        out_ref[:, j, :] = jnp.where(core == 0, full[0:AB], full[AB:])

    swap.wait_send()
    drain(tps.at[:, 0:3], t_ss)
    drain(wb.at[0:7], w_ss)
    drain(msg.at[:, 0 : NCHIP - 1], m_ss)
    drain(rxa, f_ss)
    drain(spa.at[0:3], a_ss)
    drain(rsb.at[0:7], b_ss)
    drain(s2a.at[0:7], c_ss)
    drain(s2b.at[0:3], d_ss)


def packed_shards(amplitudes, integrals, occ_irrep, vir_irrep):
    t = amplitudes.reshape(ITILE * AB * KB, V)
    w = integrals.reshape(KB * AB, J, V)
    vm = pltpu.VMEM
    dma = pltpu.SemaphoreType.DMA
    out, fits = pl.pallas_call(
        kernel,
        out_shape=(jax.ShapeDtypeStruct((AB, J, V), F32), jax.ShapeDtypeStruct((1, 1), F32)),
        in_specs=[pl.BlockSpec(memory_space=pl.ANY)] * 2 + [pl.BlockSpec(memory_space=vm)] * 2,
        out_specs=(pl.BlockSpec(memory_space=vm), pl.BlockSpec(memory_space=pltpu.SMEM)),
        scratch_shapes=[
            vm((V, V), BF16), vm((KB * AB, J, V), BF16),
            vm((V, 256), BF16), vm((V, 128), I32), vm((V, 128), I32), vm((8, V), I32), vm((V, 256), BF16), vm((V, 256), BF16),
            vm((3, ITILE, 6, KB, 128), BF16), vm((3, 6, NX, KB, 128), BF16), vm((4 * O, 256), BF16),
            vm((J, KB * AB * 3 // 2, 128), BF16), vm((2 * NX, KB * AB * 3 // 2, 128), BF16), vm((2, V, 256), BF16),
            vm((2, V, 128), F32), vm((8 * NCHIP, V), BF16), vm((NCHIP * 16, 128), F32),
            vm((3, NCHIP, 16, 128), BF16), vm((3, NCHIP, 16, 128), BF16), vm((3, NCHIP, 16, 128), BF16),
            vm((2 * NCHIP * 48, 128), F32),
            vm((V, 1024), BF16), vm((V, 1024), BF16),
            vm((192, 128), F32), vm((4, 192, 128), F32), vm((8 * 48, 128), F32), vm((4, 192, 128), F32), vm((8, 48, 128), F32),
            vm((8, 24, 128), F32), vm((48, 128), F32), vm((4, 16, 128), F32), vm((8, 24, 128), F32), vm((4, 16, 128), F32),
            vm((40, 128), F32), vm((40, 128), F32), vm((J, 24, 128), F32),
            dma, dma, dma, dma((3,)), dma, dma, dma, dma((3,)), dma, dma((3,)),
            dma, dma, dma, dma, dma, dma, dma, dma, dma, dma,
        ],
        compiler_params=pltpu.CompilerParams(
            collective_id=0, has_side_effects=True, vmem_limit_bytes=62 * 1024 * 1024
        ),
        cost_estimate=pl.CostEstimate(flops=6_000_000_000, bytes_accessed=4_000_000, transcendentals=0),
    )(t, w, occ_irrep.reshape(1, O), vir_irrep.reshape(6, 128))
    return out[None], fits[0, 0]


def shards(amplitudes, integrals, occ_irrep, vir_irrep):
    packed, fits = packed_shards(amplitudes, integrals, occ_irrep, vir_irrep)
    return lax.cond(
        fits > 0.5,
        lambda *args: packed,
        dense_shards,
        amplitudes,
        integrals,
        occ_irrep,
        vir_irrep,
    )


def solution(mesh):
    return jax.shard_map(
        shards,
        mesh=mesh,
        in_specs=(P(None, "amp", "ctr", None), P("ctr", "amp", None, None), P(), P()),
        out_specs=P("ctr", "amp", None, None),
        check_vma=False,
    )
```

```python
import functools

import jax
import jax.numpy as jnp
from jax import lax
from jax.experimental import pallas as pl
from jax.experimental.pallas import tpu as pltpu
from jax.sharding import PartitionSpec as P

O, V, ITILE, J = 64, 768, 4, 2
NX, NCHIP, AB = 4, 32, 12
KB = O // NX
CAPB = 192
CAPK = 21
MESH = pl.DeviceIdType.MESH
F32, BF16, I32 = jnp.float32, jnp.bfloat16, jnp.int32
NT = (((1,), (1,)), ((), ()))


def dense_shards(amplitudes, integrals, occ_irrep, vir_irrep):
    regrouped = lax.all_to_all(
        lax.all_to_all(amplitudes, "amp", split_axis=3, concat_axis=1, tiled=True),
        "ctr",
        split_axis=0,
        concat_axis=2,
        tiled=True,
    )
    own_rows, vir_full, occ_full, vir_local = regrouped.shape
    tile_size = own_rows * lax.axis_size("ctr")
    pair_count = integrals.shape[2]
    vir_block = lax.dynamic_slice_in_dim(vir_irrep, lax.axis_index("amp") * vir_local, vir_local)
    occ_tile = lax.dynamic_slice_in_dim(occ_irrep, lax.axis_index("ctr") * own_rows, own_rows)
    pair_labels = lax.dynamic_slice_in_dim(occ_irrep, tile_size, pair_count)
    t_left = jnp.bitwise_xor(occ_tile[:, None, None, None], vir_irrep[None, :, None, None])
    t_right = jnp.bitwise_xor(occ_irrep[None, None, :, None], vir_block[None, None, None, :])
    masked_amps = jnp.where(t_left == t_right, regrouped, jnp.zeros_like(regrouped))
    amp_matrix = masked_amps.reshape(own_rows * vir_full, occ_full * vir_local)
    w_right = jnp.bitwise_xor(pair_labels[None, None, :, None], vir_irrep[None, None, None, :])
    copies = jnp.broadcast_to(integrals[None], (lax.axis_size("ctr"),) + integrals.shape)
    integral_block = lax.all_to_all(copies, "ctr", split_axis=0, concat_axis=0, tiled=True)
    integral_block = integral_block.reshape((-1,) + integrals.shape[1:])
    count = integral_block.shape[0]
    w_left = jnp.bitwise_xor(occ_irrep[:, None, None, None], vir_block[None, :, None, None])
    w_masked = jnp.where(w_left == w_right, integral_block, jnp.zeros_like(integral_block))
    w_matrix = w_masked.reshape(count * vir_local, pair_count * vir_full)
    partial_value = jnp.dot(amp_matrix, w_matrix, preferred_element_type=jnp.float32)
    partial_value = partial_value.reshape(own_rows, vir_full, pair_count, vir_full)
    pieces = partial_value.reshape(lax.axis_size("amp"), own_rows, vir_local, pair_count, vir_full)
    summed = jnp.sum(lax.all_to_all(pieces, "amp", split_axis=0, concat_axis=0, tiled=True), axis=0)
    swapped = lax.all_to_all(summed, "amp", split_axis=3, concat_axis=1, tiled=True)
    return summed + jnp.transpose(swapped, (0, 3, 2, 1))


def iota(shape, dim):
    return lax.broadcasted_iota(I32, shape, dim)


def onehot(cond):
    return jnp.where(cond, 1.0, 0.0).astype(BF16)


def split2(value):
    hi = value.astype(BF16)
    return hi, (value - hi.astype(F32)).astype(BF16)


def far_first(step, size):
    move = (step + 1) // 2
    return size // 2 + jnp.where(step % 2 == 1, -move, move)


def drain(ref, sem):
    pltpu.make_async_copy(ref, ref, sem).wait()


def kernel(
    t_ref, w_ref, occ_ref, vir_ref, out_ref, fits_ref,
    tv, wv, q_ref, cols_ref, cols2_ref, rows_ref, rt_ref, rbd_ref, tps, tpr, xt, ws, wb, xw, ut, lhs6, msgf, msg, rxa, rxb, rxf,
    ls, rs, spf, spa, spb, rsa, rsb, s2a, s2f, s2b, r2a, r2b, x2s, x2r, dup,
    tv_s, wv_s,
    t_ss, t_rs, w_ss, w_rs, m_ss, m_rs, f_ss, f_rs, a_ss, a_rs, b_ss, b_rs, c_ss, c_rs, d_ss, d_rs, x_ss, x_rs,
):
    amp = lax.axis_index("amp")
    x = lax.axis_index("ctr")
    chip, core = amp // 2, amp % 2
    sib = 1 - core
    y, z = chip // 8, chip % 8

    GR = 4 * KB

    def t_in(e):
        rows = (slice(None), pl.ds(e * GR, GR))
        return pltpu.make_async_copy(t_ref.at[rows], tv.at[rows], tv_s.at[e])

    w_in = pltpu.make_async_copy(w_ref, wv, wv_s)
    for e in range(3):
        t_in(e).start()
    w_in.start()
    barrier = pltpu.get_barrier_semaphore()

    def partner(d):
        yy = lax.rem(y + far_first(d % 4, 4), 4)
        zz = lax.rem(z + far_first(d // 4, 8), 8)
        return yy * 8 + zz

    @pl.loop(0, NCHIP - 1)
    def _(d):
        pl.semaphore_signal(barrier, inc=1, device_id=(partner(d) * 2 + core, x), device_id_type=MESH)

    XFAR, YFAR, ZFAR = (2, 1, 3), (2, 1, 3), (4, 3, 5, 2, 6, 1, 7)
    GROUP = [(d, c) for d in XFAR for c in (core, sib)] + [(0, sib)]
    for d, cc in GROUP:
        pl.semaphore_signal(barrier, inc=1, device_id=(chip * 2 + cc, lax.rem(x + d, NX)), device_id_type=MESH)

    vrow = jnp.concatenate([vir_ref[r : r + 1, :] for r in range(6)], axis=1)
    occ8 = jnp.broadcast_to(jnp.concatenate([occ_ref[...], jnp.zeros((1, 128 - O), I32)], axis=1), (8, 128))
    occ_i = [occ8[0:1, r : r + 1] for r in range(ITILE)]
    occ_j = [occ8[0:1, ITILE + r : ITILE + r + 1] for r in range(J)]
    own_i = jnp.where(x < 2, jnp.where(x == 0, occ_i[0], occ_i[1]), jnp.where(x == 2, occ_i[2], occ_i[3]))
    own_j = jnp.where(core == 0, occ_j[0], occ_j[1])
    occ_sq = jnp.broadcast_to(occ8[0:1, :], (128, 128))
    occ_cl = occ_sq.T
    r0, r1 = iota((128, 128), 0), iota((128, 128), 1)
    rank_k = jnp.sum(jnp.where((occ_sq == occ_cl) & (r0 < r1) & (r0 < O), 1.0, 0.0), axis=0, keepdims=True)
    picked = onehot(iota((V, 128), 0) == chip * 2 * AB + iota((V, 128), 1))
    vrow8 = jnp.broadcast_to(vrow, (8, V))
    vchip = jnp.dot(vrow8.astype(F32).astype(BF16), picked, preferred_element_type=F32)
    sub8 = iota((8, 128), 0)
    table = jnp.where(
        sub8 == 0,
        occ8.astype(F32),
        jnp.where(sub8 == 1, vchip, jnp.broadcast_to(rank_k, (8, 128))),
    ).astype(BF16)
    lane = iota((1, V), 1)
    deep = iota((128, V), 0)

    def expand(index):
        return jnp.dot(table, onehot(deep == index), preferred_element_type=F32).astype(I32)

    def occ_at(e):
        return e[0:1]

    def vir_at(e):
        return e[1:2]

    def rank_at(e):
        return e[2:3]

    lane_i = lane // (AB * KB)
    lab_i = jnp.where(lane_i < 2, jnp.where(lane_i == 0, occ_i[0], occ_i[1]), jnp.where(lane_i == 2, occ_i[2], occ_i[3]))
    row_t = lab_i ^ occ_at(expand(x * KB + lane % KB)) ^ vir_at(expand(core * AB + (lane % (AB * KB)) // KB))
    rows_ref[3:4, :] = vrow
    cols_ref[...] = jnp.concatenate([jnp.concatenate([row_t, vrow, vrow, vrow], axis=0)] * 32, axis=0).T
    lower = onehot(r0 > r1)
    passed = jnp.zeros((1, 128), F32)
    top = jnp.zeros((1, 1), I32)
    slot = iota((128, 256), 1)
    slot = jnp.where(slot < CAPB, slot, slot - 64)
    for blk in range(6):
        same = jnp.where(cols_ref[blk * 128 : (blk + 1) * 128, 1:2] == r1, 1.0, 0.0)
        counts = jnp.dot(lower, same.astype(BF16), preferred_element_type=F32) + passed
        rank = jnp.sum(counts * same, axis=1, keepdims=True).astype(I32)
        passed = passed + jnp.sum(same, axis=0, keepdims=True)
        q_ref[blk * 128 : (blk + 1) * 128, :] = onehot(rank == slot)
    low = jnp.max(passed, axis=1, keepdims=True) <= CAPB
    fits = low & (jnp.max(jnp.where(r1[0:1, :] < O, rank_k, 0.0), axis=1, keepdims=True) < CAPK)
    fits_ref[0, 0] = jnp.max(jnp.where(fits, 1.0, 0.0))

    left = iota((1, 128), 1) < 64
    half0, half1 = onehot(left), onehot(jnp.logical_not(left))

    def pair_up(first, second):
        return jnp.where(left, first, second)

    def t_copy(e, xx, slot):
        return pltpu.make_async_remote_copy(
            src_ref=tps.at[e, xx], dst_ref=tpr.at[e, :, slot], send_sem=t_ss, recv_sem=t_rs.at[e],
            device_id=(amp, xx), device_id_type=MESH,
        )

    for e in range(3):
        t_in(e).wait()
        pieces = []
        for i in range(ITILE):
            start = i * AB * KB + e * GR
            keep = cols_ref[start : start + GR, 0:1] == rows_ref[3:4, :]
            pieces.append(jnp.where(keep, tv[i, e * GR : (e + 1) * GR, :].astype(F32), 0.0).astype(BF16))
        packed = jnp.dot(jnp.concatenate(pieces, axis=0), q_ref[...], preferred_element_type=F32)
        for i in range(ITILE):
            start = i * GR
            tps[e, i, 0:4] = packed[start : start + GR, 0:128].astype(BF16).reshape(4, KB, 128)
            tail = pair_up(packed[start : start + GR // 2, 128:], packed[start + GR // 2 : start + GR, 128:])
            tps[e, i, 4:] = tail.astype(BF16).reshape(2, KB, 128)
        if e == 0:
            pl.semaphore_wait(barrier, NCHIP - 1 + 7)
        for d in XFAR:
            t_copy(e, lax.rem(x + d, NX), x).start()
        tpr[e, :, x] = tps[e, x]

    e_k = expand(lane % O)
    row_ak = own_i ^ occ_at(e_k) ^ vir_at(expand(core * AB + lane // O))
    e_kc = expand(lane // AB)
    c0 = vir_at(expand(lane % AB))
    c1 = vir_at(expand(AB + lane % AB))
    row_w = occ_at(expand(x * KB + lane // AB)) ^ jnp.where(core == 0, c0, c1)
    chip_c = jnp.where(lane < AB, c0, c1)
    rows_ref[0:1, :] = row_ak
    rows_ref[1:2, :] = occ_at(e_kc) ^ c0 ^ own_j
    rows_ref[2:3, :] = occ_at(e_kc) ^ c1 ^ own_j
    stack = jnp.concatenate([row_w, rank_at(e_k), rank_at(e_kc), chip_c], axis=0)
    cols2_ref[...] = jnp.concatenate([stack] * 32, axis=0).T

    w_in.wait()
    for j in range(J):
        keep = (cols2_ref[0 : KB * AB, 0:1] ^ occ_j[j]) == rows_ref[3:4, :]
        masked = jnp.where(keep, wv[:, j, :].astype(F32), 0.0).astype(BF16)
        packed = jnp.dot(masked, q_ref[...], preferred_element_type=F32)
        half = AB * KB // 2
        ws[j, 0 : 2 * half] = packed[:, 0:128].astype(BF16)
        ws[j, 2 * half :] = pair_up(packed[0:half, 128:], packed[half:, 128:]).astype(BF16)

    def w_copy(xx, cc, slot_x, slot_c):
        return pltpu.make_async_remote_copy(
            src_ref=ws.at[cc], dst_ref=wb.at[slot_c * NX + slot_x], send_sem=w_ss, recv_sem=w_rs,
            device_id=(chip * 2 + cc, xx), device_id_type=MESH,
        )

    for d, cc in GROUP:
        w_copy(lax.rem(x + d, NX), cc, x, core).start()
    wb[core * NX + x] = ws[core]

    pair = iota((V, 256), 1)
    inner = pair % 128
    deep_t = iota((V, 256), 0)
    rt_ref[...] = onehot(
        (inner // CAPK == deep_t // 128)
        & (pair // 128 == (deep_t % 128) // O)
        & (inner % CAPK == cols2_ref[:, 1:2])
        & (inner < 6 * CAPK)
    )
    rbd_ref[...] = onehot(
        ((pair // 128) * 6 + inner // CAPK == deep_t % AB)
        & (inner % CAPK == cols2_ref[:, 2:3])
        & (inner < 6 * CAPK)
    )

    def m_copy(e, q, slot):
        return pltpu.make_async_remote_copy(
            src_ref=msg.at[e, q], dst_ref=rxa.at[e, slot], send_sem=m_ss, recv_sem=m_rs.at[e],
            device_id=(q * 2 + core, x), device_id_type=MESH,
        )

    def f_copy(e):
        return pltpu.make_async_remote_copy(
            src_ref=rxa.at[e], dst_ref=rxb.at[e], send_sem=f_ss, recv_sem=f_rs.at[e],
            device_id=(chip * 2 + sib, x), device_id_type=MESH,
        )

    for e in range(3):
        drain(tpr.at[e, :, 0:3], t_rs.at[e])
        xt[:, 0:128] = tpr[e, 0:4].reshape(4 * O, 128)
        both = tpr[e, 4:].reshape(2 * O, 128)
        xt[0 : 2 * O, 128:] = both * half0
        xt[2 * O :, 128:] = both * half1
        full = lax.dot_general(q_ref[...], xt[...], NT, preferred_element_type=F32)
        full = jnp.where(cols_ref[:, 1:2] == rows_ref[0:1, e * 256 : (e + 1) * 256], full, 0.0)
        for t in range(2):
            ut[t] = full[:, t * 128 : (t + 1) * 128]
        for g in range(4):
            for t in range(2):
                for c6 in range(6):
                    piece = ut[t, pl.ds(g * 6 + c6, NCHIP, stride=24), :]
                    base = (g * 2 + t) * NCHIP
                    lhs6[base : base + NCHIP, c6 * 128 : (c6 + 1) * 128] = piece.astype(BF16)
        packed = jnp.dot(lhs6[...], rt_ref[...], preferred_element_type=F32)
        for g in range(4):
            for t in range(2):
                for a2 in range(2):
                    base = (g * 2 + t) * NCHIP
                    msgf[pl.ds((2 * t + a2) * 4 + g, NCHIP, stride=16), :] = packed[
                        base : base + NCHIP, a2 * 128 : (a2 + 1) * 128
                    ]
        msg[e] = msgf[...].astype(BF16).reshape(NCHIP, 16, 128)

        @pl.loop(0, NCHIP - 1)
        def _(d):
            m_copy(e, partner(d), chip).start()

        rxa[e, chip] = msg[e, chip]

    drain(wb.at[0:7], w_rs)
    for c in range(2):
        for xx in range(NX):
            base = xx * AB * KB
            half = AB * KB // 2
            xw[c, base : base + 2 * half, 0:128] = wb[c * NX + xx, 0 : 2 * half]
            xw[c, base : base + half, 128:] = wb[c * NX + xx, 2 * half :] * half0
            xw[c, base + half : base + 2 * half, 128:] = wb[c * NX + xx, 2 * half :] * half1

    @pl.loop(0, 3)
    def _(m):
        rows = pl.ds(pl.multiple_of(m * 256, 256), 256)
        for c in range(2):
            full = lax.dot_general(q_ref[rows, :], xw[c], NT, preferred_element_type=F32)
            full = jnp.where(cols_ref[rows, 1:2] == rows_ref[1 + c : 2 + c, :], full, 0.0).astype(BF16)
            packed = jnp.dot(full, rbd_ref[...], preferred_element_type=F32).astype(BF16)
            ls[rows, 512 + c * 256 : 768 + c * 256] = packed
            rs[rows, c * 256 : (c + 1) * 256] = packed

    for e in range(3):
        drain(rxa.at[e, 0 : NCHIP - 1], m_rs.at[e])
        f_copy(e).start()

        @pl.loop(0, NCHIP)
        def _(q):
            rxf[pl.ds(pl.multiple_of((q * 2 + core) * 48 + e * 16, 16), 16), :] = rxa[e, q].astype(F32)

    for e in range(3):
        drain(rxb.at[e], f_rs.at[e])

        @pl.loop(0, NCHIP)
        def _(q):
            rxf[pl.ds(pl.multiple_of((q * 2 + sib) * 48 + e * 16, 16), 16), :] = rxb[e, q].astype(F32)

    for g in range(4):
        piece = rxf[pl.ds(g, V, stride=4), :].astype(BF16)
        ls[:, g * 128 : (g + 1) * 128] = piece
        rs[:, 512 + g * 128 : 640 + g * 128] = piece

    def a_copy(yy, slot):
        return pltpu.make_async_remote_copy(
            src_ref=spa.at[yy], dst_ref=rsa.at[slot], send_sem=a_ss, recv_sem=a_rs,
            device_id=((yy * 8 + z) * 2 + core, x), device_id_type=MESH,
        )

    def b_copy(h, zz, slot):
        return pltpu.make_async_remote_copy(
            src_ref=spb.at[h, pl.ds(pl.multiple_of(zz * 24, 24), 24)], dst_ref=rsb.at[h, slot],
            send_sem=b_ss, recv_sem=b_rs.at[h],
            device_id=((y * 8 + zz) * 2 + core, x), device_id_type=MESH,
        )

    def c_copy(zz, slot):
        return pltpu.make_async_remote_copy(
            src_ref=s2a.at[zz], dst_ref=r2a.at[slot], send_sem=c_ss, recv_sem=c_rs,
            device_id=((y * 8 + zz) * 2 + core, x), device_id_type=MESH,
        )

    def d_copy(yy, slot):
        return pltpu.make_async_remote_copy(
            src_ref=s2b.at[yy], dst_ref=r2b.at[slot], send_sem=d_ss, recv_sem=d_rs,
            device_id=((yy * 8 + z) * 2 + core, x), device_id_type=MESH,
        )

    for turn, step in enumerate(YFAR + (0,)):
        yy = lax.rem(y + step, 4)
        rows = pl.ds(pl.multiple_of(yy * 192, 192), 192)
        full = lax.dot_general(ls[rows, :], rs[...], NT, preferred_element_type=F32)
        keep = cols_ref[rows, 1:2] == (rows_ref[3:4, :] ^ (own_i ^ own_j))
        hi, lo = split2(jnp.where(keep, full, 0.0))
        packed = jnp.dot(hi, q_ref[...], preferred_element_type=F32)
        packed += jnp.dot(lo, q_ref[...], preferred_element_type=F32)
        spa[yy] = packed[:, 0:128]
        if step > 0:
            a_copy(yy, y).start()
        spf[...] = packed[:, 128:]
        paired = pair_up(spf[pl.ds(0, 96, stride=2), :], spf[pl.ds(1, 96, stride=2), :])
        spb[turn // 2, pl.ds(turn % 2, 96, stride=2), :] = paired
        if turn % 2 == 1:
            for d in ZFAR:
                b_copy(turn // 2, lax.rem(z + d, 8), z).start()
            rsb[turn // 2, z] = spb[turn // 2, pl.ds(pl.multiple_of(z * 24, 24), 24), :]

    rsa[y] = spa[y]
    drain(rsa.at[0:3], a_rs)
    s2a[...] = jnp.sum(rsa[...], axis=0).reshape(8, 24, 128)
    for d in ZFAR:
        c_copy(lax.rem(z + d, 8), z).start()
    r2a[z] = s2a[z]
    for turn, step in enumerate(YFAR + (0,)):
        if turn % 2 == 0:
            drain(rsb.at[turn // 2, 0:7], b_rs.at[turn // 2])
            s2f[turn // 2] = jnp.sum(rsb[turn // 2], axis=0)
        part = s2f[turn // 2, pl.ds(turn % 2, 12, stride=2), :]
        s2b[lax.rem(y + step, 4)] = jnp.concatenate([part, jnp.zeros((4, 128), F32)], axis=0)
    for d in YFAR:
        d_copy(lax.rem(y + d, 4), y).start()
    r2b[y] = s2b[y]
    drain(r2a.at[0:7], c_rs)
    drain(r2b.at[0:3], d_rs)

    x2s[0:24, :] = jnp.sum(r2a[...], axis=0)
    x2s[24:40, :] = jnp.sum(r2b[...], axis=0)
    swap = pltpu.make_async_remote_copy(
        src_ref=x2s, dst_ref=x2r, send_sem=x_ss, recv_sem=x_rs, device_id=(chip * 2 + sib, x), device_id_type=MESH
    )
    swap.start()
    swap.wait_recv()
    parts = []
    for j in range(J):
        own = jnp.where(core == j, x2s[...], x2r[...])
        tail = own[24:36]
        dup[j, pl.ds(0, AB, stride=2), :] = jnp.where(left, tail, 0.0)
        dup[j, pl.ds(1, AB, stride=2), :] = jnp.where(left, 0.0, tail)
        joint = jnp.concatenate([own[0:24], dup[j]], axis=1)
        hi = joint.astype(BF16).astype(F32)
        parts += [hi, joint - hi]
    parts = jnp.concatenate(parts, axis=0).astype(BF16)
    spread = lax.dot_general(parts, q_ref[...], NT, preferred_element_type=F32)
    for j in range(J):
        full = spread[j * 48 : j * 48 + 24] + spread[j * 48 + 24 : j * 48 + 48]
        keep = cols2_ref[0:24, 3:4] == (rows_ref[3:4, :] ^ (own_i ^ occ_j[j]))
        full = jnp.where(keep, full, 0.0)
        out_ref[:, j, :] = jnp.where(core == 0, full[0:AB], full[AB:])

    swap.wait_send()
    drain(tps.at[:, 0:3], t_ss)
    drain(wb.at[0:7], w_ss)
    drain(msg.at[:, 0 : NCHIP - 1], m_ss)
    drain(rxa, f_ss)
    drain(spa.at[0:3], a_ss)
    drain(rsb.at[:, 0:7], b_ss)
    drain(s2a.at[0:7], c_ss)
    drain(s2b.at[0:3], d_ss)


def packed_shards(amplitudes, integrals, occ_irrep, vir_irrep):
    t = amplitudes.reshape(ITILE, AB * KB, V)
    w = integrals.reshape(KB * AB, J, V)
    vm = pltpu.VMEM
    dma = pltpu.SemaphoreType.DMA
    out, fits = pl.pallas_call(
        kernel,
        out_shape=(jax.ShapeDtypeStruct((AB, J, V), F32), jax.ShapeDtypeStruct((1, 1), F32)),
        in_specs=[pl.BlockSpec(memory_space=pl.ANY)] * 2 + [pl.BlockSpec(memory_space=vm)] * 2,
        out_specs=(pl.BlockSpec(memory_space=vm), pl.BlockSpec(memory_space=pltpu.SMEM)),
        scratch_shapes=[
            vm((ITILE, AB * KB, V), BF16), vm((KB * AB, J, V), BF16),
            vm((V, 256), BF16), vm((V, 128), I32), vm((V, 128), I32), vm((8, V), I32), vm((V, 256), BF16), vm((V, 256), BF16),
            vm((3, ITILE, 6, KB, 128), BF16), vm((3, 6, NX, KB, 128), BF16), vm((4 * O, 256), BF16),
            vm((J, KB * AB * 3 // 2, 128), BF16), vm((2 * NX, KB * AB * 3 // 2, 128), BF16), vm((2, V, 256), BF16),
            vm((2, V, 128), F32), vm((8 * NCHIP, V), BF16), vm((NCHIP * 16, 128), F32),
            vm((3, NCHIP, 16, 128), BF16), vm((3, NCHIP, 16, 128), BF16), vm((3, NCHIP, 16, 128), BF16),
            vm((2 * NCHIP * 48, 128), F32),
            vm((V, 1024), BF16), vm((V, 1024), BF16),
            vm((192, 128), F32), vm((4, 192, 128), F32), vm((2, 8 * 24, 128), F32), vm((4, 192, 128), F32), vm((2, 8, 24, 128), F32),
            vm((8, 24, 128), F32), vm((2, 24, 128), F32), vm((4, 16, 128), F32), vm((8, 24, 128), F32), vm((4, 16, 128), F32),
            vm((40, 128), F32), vm((40, 128), F32), vm((J, 24, 128), F32),
            dma((3,)), dma, dma, dma((3,)), dma, dma, dma, dma((3,)), dma, dma((3,)),
            dma, dma, dma, dma((2,)), dma, dma, dma, dma, dma, dma,
        ],
        compiler_params=pltpu.CompilerParams(
            collective_id=0, has_side_effects=True, vmem_limit_bytes=62 * 1024 * 1024
        ),
        cost_estimate=pl.CostEstimate(flops=6_000_000_000, bytes_accessed=4_000_000, transcendentals=0),
    )(t, w, occ_irrep.reshape(1, O), vir_irrep.reshape(6, 128))
    return out[None], fits[0, 0]


def shards(amplitudes, integrals, occ_irrep, vir_irrep):
    packed, fits = packed_shards(amplitudes, integrals, occ_irrep, vir_irrep)
    return lax.cond(
        fits > 0.5,
        lambda *args: packed,
        dense_shards,
        amplitudes,
        integrals,
        occ_irrep,
        vir_irrep,
    )


def solution(mesh):
    return jax.shard_map(
        shards,
        mesh=mesh,
        in_specs=(P(None, "amp", "ctr", None), P("ctr", "amp", None, None), P(), P()),
        out_specs=P("ctr", "amp", None, None),
        check_vma=False,
    )
```

```python
import functools

import jax
import jax.numpy as jnp
from jax import lax
from jax.experimental import pallas as pl
from jax.experimental.pallas import tpu as pltpu
from jax.sharding import PartitionSpec as P

O, V, ITILE, J = 64, 768, 4, 2
NX, NCHIP, AB = 4, 32, 12
KB = O // NX
CAPB = 192
CAPK = 21
MESH = pl.DeviceIdType.MESH
F32, BF16, I32 = jnp.float32, jnp.bfloat16, jnp.int32
NT = (((1,), (1,)), ((), ()))


def dense_shards(amplitudes, integrals, occ_irrep, vir_irrep):
    regrouped = lax.all_to_all(
        lax.all_to_all(amplitudes, "amp", split_axis=3, concat_axis=1, tiled=True),
        "ctr",
        split_axis=0,
        concat_axis=2,
        tiled=True,
    )
    own_rows, vir_full, occ_full, vir_local = regrouped.shape
    tile_size = own_rows * lax.axis_size("ctr")
    pair_count = integrals.shape[2]
    vir_block = lax.dynamic_slice_in_dim(vir_irrep, lax.axis_index("amp") * vir_local, vir_local)
    occ_tile = lax.dynamic_slice_in_dim(occ_irrep, lax.axis_index("ctr") * own_rows, own_rows)
    pair_labels = lax.dynamic_slice_in_dim(occ_irrep, tile_size, pair_count)
    t_left = jnp.bitwise_xor(occ_tile[:, None, None, None], vir_irrep[None, :, None, None])
    t_right = jnp.bitwise_xor(occ_irrep[None, None, :, None], vir_block[None, None, None, :])
    masked_amps = jnp.where(t_left == t_right, regrouped, jnp.zeros_like(regrouped))
    amp_matrix = masked_amps.reshape(own_rows * vir_full, occ_full * vir_local)
    w_right = jnp.bitwise_xor(pair_labels[None, None, :, None], vir_irrep[None, None, None, :])
    copies = jnp.broadcast_to(integrals[None], (lax.axis_size("ctr"),) + integrals.shape)
    integral_block = lax.all_to_all(copies, "ctr", split_axis=0, concat_axis=0, tiled=True)
    integral_block = integral_block.reshape((-1,) + integrals.shape[1:])
    count = integral_block.shape[0]
    w_left = jnp.bitwise_xor(occ_irrep[:, None, None, None], vir_block[None, :, None, None])
    w_masked = jnp.where(w_left == w_right, integral_block, jnp.zeros_like(integral_block))
    w_matrix = w_masked.reshape(count * vir_local, pair_count * vir_full)
    partial_value = jnp.dot(amp_matrix, w_matrix, preferred_element_type=jnp.float32)
    partial_value = partial_value.reshape(own_rows, vir_full, pair_count, vir_full)
    pieces = partial_value.reshape(lax.axis_size("amp"), own_rows, vir_local, pair_count, vir_full)
    summed = jnp.sum(lax.all_to_all(pieces, "amp", split_axis=0, concat_axis=0, tiled=True), axis=0)
    swapped = lax.all_to_all(summed, "amp", split_axis=3, concat_axis=1, tiled=True)
    return summed + jnp.transpose(swapped, (0, 3, 2, 1))


def iota(shape, dim):
    return lax.broadcasted_iota(I32, shape, dim)


def onehot(cond):
    return jnp.where(cond, 1.0, 0.0).astype(BF16)


def split2(value):
    hi = value.astype(BF16)
    return hi, (value - hi.astype(F32)).astype(BF16)


def far_first(step, size):
    move = (step + 1) // 2
    return size // 2 + jnp.where(step % 2 == 1, -move, move)


def drain(ref, sem):
    pltpu.make_async_copy(ref, ref, sem).wait()


def kernel(
    t_ref, w_ref, occ_ref, vir_ref, out_ref, fits_ref,
    tv, wv, q_ref, cols_ref, cols2_ref, rows_ref, rt_ref, rbd_ref, tps, tpr, xt, ws, wb, xw, ut, lhs6, msgf, msg, rxa, rxb, rxf,
    ls, rs, spf, spa, spb, rsa, rsb, s2a, s2f, s2b, r2a, r2b, x2s, x2r, dup,
    tv_s, wv_s,
    t_ss, t_rs, w_ss, w_rs, m_ss, m_rs, f_ss, f_rs, a_ss, a_rs, b_ss, b_rs, c_ss, c_rs, d_ss, d_rs, x_ss, x_rs,
):
    amp = lax.axis_index("amp")
    x = lax.axis_index("ctr")
    chip, core = amp // 2, amp % 2
    sib = 1 - core
    y, z = chip // 8, chip % 8

    GR = 4 * KB

    def t_in(e):
        rows = (slice(None), pl.ds(e * GR, GR))
        return pltpu.make_async_copy(t_ref.at[rows], tv.at[rows], tv_s.at[e])

    w_in = pltpu.make_async_copy(w_ref, wv, wv_s)
    for e in range(3):
        t_in(e).start()
    w_in.start()
    barrier = pltpu.get_barrier_semaphore()

    def partner(d):
        yy = lax.rem(y + far_first(d % 4, 4), 4)
        zz = lax.rem(z + far_first(d // 4, 8), 8)
        return yy * 8 + zz

    @pl.loop(0, NCHIP - 1)
    def _(d):
        pl.semaphore_signal(barrier, inc=1, device_id=(partner(d) * 2 + core, x), device_id_type=MESH)

    XFAR, YFAR, ZFAR = (2, 1, 3), (2, 1, 3), (4, 3, 5, 2, 6, 1, 7)
    GROUP = [(d, c) for d in XFAR for c in (core, sib)] + [(0, sib)]
    for d, cc in GROUP:
        pl.semaphore_signal(barrier, inc=1, device_id=(chip * 2 + cc, lax.rem(x + d, NX)), device_id_type=MESH)

    vrow = jnp.concatenate([vir_ref[r : r + 1, :] for r in range(6)], axis=1)
    occ8 = jnp.broadcast_to(jnp.concatenate([occ_ref[...], jnp.zeros((1, 128 - O), I32)], axis=1), (8, 128))
    occ_i = [occ8[0:1, r : r + 1] for r in range(ITILE)]
    occ_j = [occ8[0:1, ITILE + r : ITILE + r + 1] for r in range(J)]
    own_i = jnp.where(x < 2, jnp.where(x == 0, occ_i[0], occ_i[1]), jnp.where(x == 2, occ_i[2], occ_i[3]))
    own_j = jnp.where(core == 0, occ_j[0], occ_j[1])
    occ_sq = jnp.broadcast_to(occ8[0:1, :], (128, 128))
    occ_cl = occ_sq.T
    r0, r1 = iota((128, 128), 0), iota((128, 128), 1)
    rank_k = jnp.sum(jnp.where((occ_sq == occ_cl) & (r0 < r1) & (r0 < O), 1.0, 0.0), axis=0, keepdims=True)
    picked = onehot(iota((V, 128), 0) == chip * 2 * AB + iota((V, 128), 1))
    vrow8 = jnp.broadcast_to(vrow, (8, V))
    vchip = jnp.dot(vrow8.astype(F32).astype(BF16), picked, preferred_element_type=F32)
    sub8 = iota((8, 128), 0)
    table = jnp.where(
        sub8 == 0,
        occ8.astype(F32),
        jnp.where(sub8 == 1, vchip, jnp.broadcast_to(rank_k, (8, 128))),
    ).astype(BF16)
    lane = iota((1, V), 1)
    deep = iota((128, V), 0)

    def expand(index):
        return jnp.dot(table, onehot(deep == index), preferred_element_type=F32).astype(I32)

    def occ_at(e):
        return e[0:1]

    def vir_at(e):
        return e[1:2]

    def rank_at(e):
        return e[2:3]

    lane_i = lane // (AB * KB)
    lab_i = jnp.where(lane_i < 2, jnp.where(lane_i == 0, occ_i[0], occ_i[1]), jnp.where(lane_i == 2, occ_i[2], occ_i[3]))
    row_t = lab_i ^ occ_at(expand(x * KB + lane % KB)) ^ vir_at(expand(core * AB + (lane % (AB * KB)) // KB))
    rows_ref[3:4, :] = vrow
    cols_ref[...] = jnp.concatenate([jnp.concatenate([row_t, vrow, vrow, vrow], axis=0)] * 32, axis=0).T
    lower = onehot(r0 > r1)
    passed = jnp.zeros((1, 128), F32)
    top = jnp.zeros((1, 1), I32)
    slot = iota((128, 256), 1)
    slot = jnp.where(slot < CAPB, slot, slot - 64)
    for blk in range(6):
        same = jnp.where(cols_ref[blk * 128 : (blk + 1) * 128, 1:2] == r1, 1.0, 0.0)
        counts = jnp.dot(lower, same.astype(BF16), preferred_element_type=F32) + passed
        rank = jnp.sum(counts * same, axis=1, keepdims=True).astype(I32)
        passed = passed + jnp.sum(same, axis=0, keepdims=True)
        q_ref[blk * 128 : (blk + 1) * 128, :] = onehot(rank == slot)
    low = jnp.max(passed, axis=1, keepdims=True) <= CAPB
    fits = low & (jnp.max(jnp.where(r1[0:1, :] < O, rank_k, 0.0), axis=1, keepdims=True) < CAPK)
    fits_ref[0, 0] = jnp.max(jnp.where(fits, 1.0, 0.0))

    left = iota((1, 128), 1) < 64
    half0, half1 = onehot(left), onehot(jnp.logical_not(left))

    def pair_up(first, second):
        return jnp.where(left, first, second)

    def t_copy(e, xx, slot):
        return pltpu.make_async_remote_copy(
            src_ref=tps.at[e, xx], dst_ref=tpr.at[e, :, slot], send_sem=t_ss, recv_sem=t_rs.at[e],
            device_id=(amp, xx), device_id_type=MESH,
        )

    for e in range(3):
        t_in(e).wait()
        pieces = []
        for i in range(ITILE):
            start = i * AB * KB + e * GR
            keep = cols_ref[start : start + GR, 0:1] == rows_ref[3:4, :]
            pieces.append(jnp.where(keep, tv[i, e * GR : (e + 1) * GR, :].astype(F32), 0.0).astype(BF16))
        packed = jnp.dot(jnp.concatenate(pieces, axis=0), q_ref[...], preferred_element_type=F32)
        for i in range(ITILE):
            start = i * GR
            tps[e, i, 0:4] = packed[start : start + GR, 0:128].astype(BF16).reshape(4, KB, 128)
            tail = pair_up(packed[start : start + GR // 2, 128:], packed[start + GR // 2 : start + GR, 128:])
            tps[e, i, 4:] = tail.astype(BF16).reshape(2, KB, 128)
        if e == 0:
            pl.semaphore_wait(barrier, NCHIP - 1 + 7)
        for d in XFAR:
            t_copy(e, lax.rem(x + d, NX), x).start()
        tpr[e, :, x] = tps[e, x]

    e_k = expand(lane % O)
    row_ak = own_i ^ occ_at(e_k) ^ vir_at(expand(core * AB + lane // O))
    e_kc = expand(lane // AB)
    c0 = vir_at(expand(lane % AB))
    c1 = vir_at(expand(AB + lane % AB))
    row_w = occ_at(expand(x * KB + lane // AB)) ^ jnp.where(core == 0, c0, c1)
    chip_c = jnp.where(lane < AB, c0, c1)
    rows_ref[0:1, :] = row_ak
    rows_ref[1:2, :] = occ_at(e_kc) ^ c0 ^ own_j
    rows_ref[2:3, :] = occ_at(e_kc) ^ c1 ^ own_j
    stack = jnp.concatenate([row_w, rank_at(e_k), rank_at(e_kc), chip_c], axis=0)
    cols2_ref[...] = jnp.concatenate([stack] * 32, axis=0).T

    w_in.wait()
    for j in range(J):
        keep = (cols2_ref[0 : KB * AB, 0:1] ^ occ_j[j]) == rows_ref[3:4, :]
        masked = jnp.where(keep, wv[:, j, :].astype(F32), 0.0).astype(BF16)
        packed = jnp.dot(masked, q_ref[...], preferred_element_type=F32)
        half = AB * KB // 2
        ws[j, 0 : 2 * half] = packed[:, 0:128].astype(BF16)
        ws[j, 2 * half :] = pair_up(packed[0:half, 128:], packed[half:, 128:]).astype(BF16)

    def w_copy(xx, cc, slot_x, slot_c):
        return pltpu.make_async_remote_copy(
            src_ref=ws.at[cc], dst_ref=wb.at[slot_c * NX + slot_x], send_sem=w_ss, recv_sem=w_rs,
            device_id=(chip * 2 + cc, xx), device_id_type=MESH,
        )

    for d, cc in GROUP:
        w_copy(lax.rem(x + d, NX), cc, x, core).start()
    wb[core * NX + x] = ws[core]

    pair = iota((V, 256), 1)
    inner = pair % 128
    deep_t = iota((V, 256), 0)
    rt_ref[...] = onehot(
        (inner // CAPK == deep_t // 128)
        & (pair // 128 == (deep_t % 128) // O)
        & (inner % CAPK == cols2_ref[:, 1:2])
        & (inner < 6 * CAPK)
    )
    rbd_ref[...] = onehot(
        ((pair // 128) * 6 + inner // CAPK == deep_t % AB)
        & (inner % CAPK == cols2_ref[:, 2:3])
        & (inner < 6 * CAPK)
    )

    def m_copy(e, q, slot):
        return pltpu.make_async_remote_copy(
            src_ref=msg.at[e, q], dst_ref=rxa.at[e, slot], send_sem=m_ss, recv_sem=m_rs.at[e],
            device_id=(q * 2 + core, x), device_id_type=MESH,
        )

    def f_copy(e):
        return pltpu.make_async_remote_copy(
            src_ref=rxa.at[e], dst_ref=rxb.at[e], send_sem=f_ss, recv_sem=f_rs.at[e],
            device_id=(chip * 2 + sib, x), device_id_type=MESH,
        )

    for e in range(3):
        drain(tpr.at[e, :, 0:3], t_rs.at[e])
        xt[:, 0:128] = tpr[e, 0:4].reshape(4 * O, 128)
        both = tpr[e, 4:].reshape(2 * O, 128)
        xt[0 : 2 * O, 128:] = both * half0
        xt[2 * O :, 128:] = both * half1
        full = lax.dot_general(q_ref[...], xt[...], NT, preferred_element_type=F32)
        full = jnp.where(cols_ref[:, 1:2] == rows_ref[0:1, e * 256 : (e + 1) * 256], full, 0.0)
        for t in range(2):
            ut[t] = full[:, t * 128 : (t + 1) * 128]
        for g in range(4):
            for t in range(2):
                for c6 in range(6):
                    piece = ut[t, pl.ds(g * 6 + c6, NCHIP, stride=24), :]
                    base = (g * 2 + t) * NCHIP
                    lhs6[base : base + NCHIP, c6 * 128 : (c6 + 1) * 128] = piece.astype(BF16)
        packed = jnp.dot(lhs6[...], rt_ref[...], preferred_element_type=F32)
        for g in range(4):
            for t in range(2):
                for a2 in range(2):
                    base = (g * 2 + t) * NCHIP
                    msgf[pl.ds((2 * t + a2) * 4 + g, NCHIP, stride=16), :] = packed[
                        base : base + NCHIP, a2 * 128 : (a2 + 1) * 128
                    ]
        msg[e] = msgf[...].astype(BF16).reshape(NCHIP, 16, 128)

        @pl.loop(0, NCHIP - 1)
        def _(d):
            m_copy(e, partner(d), chip).start()

        rxa[e, chip] = msg[e, chip]

    drain(wb.at[0:7], w_rs)
    for c in range(2):
        for xx in range(NX):
            base = xx * AB * KB
            half = AB * KB // 2
            xw[c, base : base + 2 * half, 0:128] = wb[c * NX + xx, 0 : 2 * half]
            xw[c, base : base + half, 128:] = wb[c * NX + xx, 2 * half :] * half0
            xw[c, base + half : base + 2 * half, 128:] = wb[c * NX + xx, 2 * half :] * half1

    @pl.loop(0, 3)
    def _(m):
        rows = pl.ds(pl.multiple_of(m * 256, 256), 256)
        for c in range(2):
            full = lax.dot_general(q_ref[rows, :], xw[c], NT, preferred_element_type=F32)
            full = jnp.where(cols_ref[rows, 1:2] == rows_ref[1 + c : 2 + c, :], full, 0.0).astype(BF16)
            packed = jnp.dot(full, rbd_ref[...], preferred_element_type=F32).astype(BF16)
            ls[rows, 512 + c * 256 : 768 + c * 256] = packed
            rs[rows, c * 256 : (c + 1) * 256] = packed

    for e in range(3):
        drain(rxa.at[e, 0 : NCHIP - 1], m_rs.at[e])
        f_copy(e).start()

        @pl.loop(0, NCHIP, unroll=8)
        def _(q):
            rxf[pl.ds(pl.multiple_of((q * 2 + core) * 48 + e * 16, 16), 16), :] = rxa[e, q].astype(F32)

    for e in range(3):
        drain(rxb.at[e], f_rs.at[e])

        @pl.loop(0, NCHIP, unroll=8)
        def _(q):
            rxf[pl.ds(pl.multiple_of((q * 2 + sib) * 48 + e * 16, 16), 16), :] = rxb[e, q].astype(F32)

    for g in range(4):
        piece = rxf[pl.ds(g, V, stride=4), :].astype(BF16)
        ls[:, g * 128 : (g + 1) * 128] = piece
        rs[:, 512 + g * 128 : 640 + g * 128] = piece

    def a_copy(yy, slot):
        return pltpu.make_async_remote_copy(
            src_ref=spa.at[yy], dst_ref=rsa.at[slot], send_sem=a_ss, recv_sem=a_rs,
            device_id=((yy * 8 + z) * 2 + core, x), device_id_type=MESH,
        )

    def b_copy(h, zz, slot):
        return pltpu.make_async_remote_copy(
            src_ref=spb.at[h, pl.ds(pl.multiple_of(zz * 24, 24), 24)], dst_ref=rsb.at[h, slot],
            send_sem=b_ss, recv_sem=b_rs.at[h],
            device_id=((y * 8 + zz) * 2 + core, x), device_id_type=MESH,
        )

    def c_copy(zz, slot):
        return pltpu.make_async_remote_copy(
            src_ref=s2a.at[zz], dst_ref=r2a.at[slot], send_sem=c_ss, recv_sem=c_rs,
            device_id=((y * 8 + zz) * 2 + core, x), device_id_type=MESH,
        )

    def d_copy(yy, slot):
        return pltpu.make_async_remote_copy(
            src_ref=s2b.at[yy], dst_ref=r2b.at[slot], send_sem=d_ss, recv_sem=d_rs,
            device_id=((yy * 8 + z) * 2 + core, x), device_id_type=MESH,
        )

    for turn, step in enumerate(YFAR + (0,)):
        yy = lax.rem(y + step, 4)
        rows = pl.ds(pl.multiple_of(yy * 192, 192), 192)
        full = lax.dot_general(ls[rows, :], rs[...], NT, preferred_element_type=F32)
        keep = cols_ref[rows, 1:2] == (rows_ref[3:4, :] ^ (own_i ^ own_j))
        hi, lo = split2(jnp.where(keep, full, 0.0))
        packed = jnp.dot(hi, q_ref[...], preferred_element_type=F32)
        packed += jnp.dot(lo, q_ref[...], preferred_element_type=F32)
        spa[yy] = packed[:, 0:128]
        if step > 0:
            a_copy(yy, y).start()
        spf[...] = packed[:, 128:]
        paired = pair_up(spf[pl.ds(0, 96, stride=2), :], spf[pl.ds(1, 96, stride=2), :])
        spb[turn // 2, pl.ds(turn % 2, 96, stride=2), :] = paired
        if turn % 2 == 1:
            for d in ZFAR:
                b_copy(turn // 2, lax.rem(z + d, 8), z).start()
            rsb[turn // 2, z] = spb[turn // 2, pl.ds(pl.multiple_of(z * 24, 24), 24), :]

    rsa[y] = spa[y]
    drain(rsa.at[0:3], a_rs)
    s2a[...] = jnp.sum(rsa[...], axis=0).reshape(8, 24, 128)
    for d in ZFAR:
        c_copy(lax.rem(z + d, 8), z).start()
    r2a[z] = s2a[z]
    for turn, step in enumerate(YFAR + (0,)):
        if turn % 2 == 0:
            drain(rsb.at[turn // 2, 0:7], b_rs.at[turn // 2])
            s2f[turn // 2] = jnp.sum(rsb[turn // 2], axis=0)
        part = s2f[turn // 2, pl.ds(turn % 2, 12, stride=2), :]
        s2b[lax.rem(y + step, 4)] = jnp.concatenate([part, jnp.zeros((4, 128), F32)], axis=0)
    for d in YFAR:
        d_copy(lax.rem(y + d, 4), y).start()
    r2b[y] = s2b[y]
    drain(r2a.at[0:7], c_rs)
    drain(r2b.at[0:3], d_rs)

    x2s[0:24, :] = jnp.sum(r2a[...], axis=0)
    x2s[24:40, :] = jnp.sum(r2b[...], axis=0)
    swap = pltpu.make_async_remote_copy(
        src_ref=x2s, dst_ref=x2r, send_sem=x_ss, recv_sem=x_rs, device_id=(chip * 2 + sib, x), device_id_type=MESH
    )
    swap.start()
    swap.wait_recv()
    parts = []
    for j in range(J):
        own = jnp.where(core == j, x2s[...], x2r[...])
        tail = own[24:36]
        dup[j, pl.ds(0, AB, stride=2), :] = jnp.where(left, tail, 0.0)
        dup[j, pl.ds(1, AB, stride=2), :] = jnp.where(left, 0.0, tail)
        joint = jnp.concatenate([own[0:24], dup[j]], axis=1)
        hi = joint.astype(BF16).astype(F32)
        parts += [hi, joint - hi]
    parts = jnp.concatenate(parts, axis=0).astype(BF16)
    spread = lax.dot_general(parts, q_ref[...], NT, preferred_element_type=F32)
    for j in range(J):
        full = spread[j * 48 : j * 48 + 24] + spread[j * 48 + 24 : j * 48 + 48]
        keep = cols2_ref[0:24, 3:4] == (rows_ref[3:4, :] ^ (own_i ^ occ_j[j]))
        full = jnp.where(keep, full, 0.0)
        out_ref[:, j, :] = jnp.where(core == 0, full[0:AB], full[AB:])

    swap.wait_send()
    drain(tps.at[:, 0:3], t_ss)
    drain(wb.at[0:7], w_ss)
    drain(msg.at[:, 0 : NCHIP - 1], m_ss)
    drain(rxa, f_ss)
    drain(spa.at[0:3], a_ss)
    drain(rsb.at[:, 0:7], b_ss)
    drain(s2a.at[0:7], c_ss)
    drain(s2b.at[0:3], d_ss)


def packed_shards(amplitudes, integrals, occ_irrep, vir_irrep):
    t = amplitudes.reshape(ITILE, AB * KB, V)
    w = integrals.reshape(KB * AB, J, V)
    vm = pltpu.VMEM
    dma = pltpu.SemaphoreType.DMA
    out, fits = pl.pallas_call(
        kernel,
        out_shape=(jax.ShapeDtypeStruct((AB, J, V), F32), jax.ShapeDtypeStruct((1, 1), F32)),
        in_specs=[pl.BlockSpec(memory_space=pl.ANY)] * 2 + [pl.BlockSpec(memory_space=vm)] * 2,
        out_specs=(pl.BlockSpec(memory_space=vm), pl.BlockSpec(memory_space=pltpu.SMEM)),
        scratch_shapes=[
            vm((ITILE, AB * KB, V), BF16), vm((KB * AB, J, V), BF16),
            vm((V, 256), BF16), vm((V, 128), I32), vm((V, 128), I32), vm((8, V), I32), vm((V, 256), BF16), vm((V, 256), BF16),
            vm((3, ITILE, 6, KB, 128), BF16), vm((3, 6, NX, KB, 128), BF16), vm((4 * O, 256), BF16),
            vm((J, KB * AB * 3 // 2, 128), BF16), vm((2 * NX, KB * AB * 3 // 2, 128), BF16), vm((2, V, 256), BF16),
            vm((2, V, 128), F32), vm((8 * NCHIP, V), BF16), vm((NCHIP * 16, 128), F32),
            vm((3, NCHIP, 16, 128), BF16), vm((3, NCHIP, 16, 128), BF16), vm((3, NCHIP, 16, 128), BF16),
            vm((2 * NCHIP * 48, 128), F32),
            vm((V, 1024), BF16), vm((V, 1024), BF16),
            vm((192, 128), F32), vm((4, 192, 128), F32), vm((2, 8 * 24, 128), F32), vm((4, 192, 128), F32), vm((2, 8, 24, 128), F32),
            vm((8, 24, 128), F32), vm((2, 24, 128), F32), vm((4, 16, 128), F32), vm((8, 24, 128), F32), vm((4, 16, 128), F32),
            vm((40, 128), F32), vm((40, 128), F32), vm((J, 24, 128), F32),
            dma((3,)), dma, dma, dma((3,)), dma, dma, dma, dma((3,)), dma, dma((3,)),
            dma, dma, dma, dma((2,)), dma, dma, dma, dma, dma, dma,
        ],
        compiler_params=pltpu.CompilerParams(
            collective_id=0, has_side_effects=True, vmem_limit_bytes=62 * 1024 * 1024
        ),
        cost_estimate=pl.CostEstimate(flops=6_000_000_000, bytes_accessed=4_000_000, transcendentals=0),
    )(t, w, occ_irrep.reshape(1, O), vir_irrep.reshape(6, 128))
    return out[None], fits[0, 0]


def shards(amplitudes, integrals, occ_irrep, vir_irrep):
    packed, fits = packed_shards(amplitudes, integrals, occ_irrep, vir_irrep)
    return lax.cond(
        fits > 0.5,
        lambda *args: packed,
        dense_shards,
        amplitudes,
        integrals,
        occ_irrep,
        vir_irrep,
    )


def solution(mesh):
    return jax.shard_map(
        shards,
        mesh=mesh,
        in_specs=(P(None, "amp", "ctr", None), P("ctr", "amp", None, None), P(), P()),
        out_specs=P("ctr", "amp", None, None),
        check_vma=False,
    )
```
